512 devices in a mesh: gy: 32 (over y_hi, z), gz: 16 (over y_lo, x, core).
Axes of the slice: x: 4, y: 4 (y_hi: 2, y_lo: 2; y = y_hi * 2 + y_lo), z: 16, core: 2. Of those that a mesh axis runs over, the one named last changes fastest.
Arguments:
- tokens: bfloat16 [2, 64, 32, 32, 1024], P(None, None, 'gy', 'gz'), may hold values from -64 to 64
- w_qkv: bfloat16 [1024, 3072], P('gy'), may hold values from -2 to 2
- w_out: bfloat16 [1024, 1024], P('gy'), may hold values from -0.1875 to 0.1875
- bias_x: float32 [16, 127], replicated, may hold values from -4 to 4
- bias_y: float32 [16, 63], replicated, may hold values from -4 to 4
- bias_z: float32 [16, 63], replicated, may hold values from -4 to 4
Outputs:
- mixed: bfloat16 [2, 64, 32, 32, 1024], P(None, None, 'gy', 'gz')
The draws below stay inside these ranges and needn't reach their ends.
All inputs are finite; a program needn't handle non-finite values.
Results may differ from the reference program's by a relative error of at most 0.0083.
Values may be sent and summed in bfloat16 or wider, within the bound.
No kernel may reach another device: no remote copies, remote signals or barrier semaphores. Data moves between devices by JAX's collectives and lax.ppermute only.
A program may use at most 64 MiB of HBM per device.

```python
import math
import jax
import jax.numpy as jnp
from jax import lax

D = 1024
HEADS = 16
HEAD = 64
SAMPLES = 2
NX = 64
NY = 32
NZ = 32


def draw_tokens(key, part):
    streams = jax.random.split(jax.random.fold_in(key, 11), 1)
    dims = (SAMPLES, NX, NY, NZ, D)
    values = jax.random.normal(streams[0], dims, jnp.float32)
    values = values * 0.25
    return jnp.clip(values, -64.0, 64.0).astype(jnp.bfloat16)


def draw_w_qkv(key, part):
    limit = 6.0 / math.sqrt(D)
    base = jax.random.normal(jax.random.fold_in(key, 12), (D, 3 * D), jnp.float32) / math.sqrt(D)
    base = jnp.clip(base, -limit, limit)
    return jnp.clip(base, -2.0, 2.0).astype(jnp.bfloat16)


def levels(stream_key, extent, cuts, smallest, top_value):
    gain, own = 1.0, jax.random.fold_in(stream_key, 6)
    for position, blocks in cuts:
        steps = jnp.exp(jax.random.uniform(jax.random.fold_in(own, position), (blocks,), jnp.float32, smallest / len(cuts), top_value / len(cuts)))
        gain = gain * jnp.repeat(steps, extent[position] // blocks).reshape([-1 if axis == position else 1 for axis in range(len(extent))])
    return gain


def normal_values(own_key, extent, scale, most, cuts=(), held_as=jnp.bfloat16):
    values = jax.random.normal(own_key, extent, jnp.float32) * scale
    if len(cuts) > 0:
        values = levels(own_key, extent, cuts, -0.22, 0.18) * values
    return jnp.clip(values, min=-most, max=most).astype(held_as)


def setup_inputs(seed: int = 0) -> dict:
    splits = jax.random.split(jax.random.key(seed), 7)
    return {
        "tokens": draw_tokens(jax.random.fold_in(splits[6], 71), 0),
        "w_qkv": draw_w_qkv(jax.random.fold_in(splits[6], 71), 0),
        "w_out": normal_values(splits[2], (D, D), D ** -0.5, 0.1875, ((0, 32),)),
        "bias_x": normal_values(splits[3], (HEADS, 2 * NX - 1), 1.0, 4.0, (), jnp.float32),
        "bias_y": normal_values(splits[4], (HEADS, 2 * NY - 1), 1.0, 4.0, (), jnp.float32),
        "bias_z": normal_values(splits[5], (HEADS, 2 * NZ - 1), 1.0, 4.0, (), jnp.float32),
    }


einsum_forms = {1: ('bxyzhs,bwyzhs->byzhxw', 'byzhxw,bwyzhs->bxyzhs'), 2: ('bxyzhs,bxwzhs->bxzhyw', 'bxzhyw,bxwzhs->bxyzhs'), 3: ('bxyzhs,bxywhs->bxyhzw', 'bxyhzw,bxywhs->bxyzhs')}

def norm_rows(tokens):
    values = tokens.astype(jnp.float32)
    center = lax.optimization_barrier(jnp.mean(values, axis=-1, keepdims=True))
    spread = lax.optimization_barrier(jnp.mean((values - center) ** 2, axis=-1, keepdims=True))
    return ((values - center) * lax.rsqrt(spread + 1e-05)).astype(jnp.bfloat16)

def rel_bias(table):
    length = (table.shape[1] + 1) // 2
    offsets = jnp.arange(length)[:, None] - jnp.arange(length)[None, :] + length - 1
    return table[:, offsets.astype(jnp.int32)]

def attend(qkv, table, axis):
    dims = qkv.shape
    features = dims[-1] // 3
    parts = qkv.reshape(dims[:-1] + (3, HEADS, HEAD))
    query = parts[..., 0, :, :].astype(jnp.float32)
    keys = parts[..., 1, :, :].astype(jnp.float32)
    values = parts[..., 2, :, :].astype(jnp.float32)
    score_form, mix_form = einsum_forms[axis]
    scores = jnp.einsum(score_form, query, keys) * HEAD ** (-0.5) + rel_bias(table)
    scores = scores - lax.optimization_barrier(jnp.max(scores, axis=-1, keepdims=True))
    expo = jnp.exp(scores)
    weights = (expo / lax.optimization_barrier(jnp.sum(expo, axis=-1, keepdims=True))).astype(jnp.bfloat16)
    mixed = jnp.einsum(mix_form, weights.astype(jnp.float32), values)
    return mixed.reshape(dims[:-1] + (features,)).astype(jnp.bfloat16)

def reference(tokens, w_qkv, w_out, bias_x, bias_y, bias_z):

    def one_sample(sample):
        normed = norm_rows(sample)
        qkv = jnp.dot(normed.reshape(-1, D), w_qkv, preferred_element_type=jnp.float32)
        qkv = qkv.astype(jnp.bfloat16).reshape((1, NX, NY, NZ, 3 * D))
        along_x = attend(qkv, bias_x, 1).astype(jnp.float32)
        along_y = attend(qkv, bias_y, 2).astype(jnp.float32)
        along_z = attend(qkv, bias_z, 3).astype(jnp.float32)
        summed = (along_x + along_y + along_z).astype(jnp.bfloat16).reshape(-1, D)
        result = jnp.dot(summed, w_out, preferred_element_type=jnp.float32)
        result = result + sample.reshape(-1, D).astype(jnp.float32)
        return result.astype(jnp.bfloat16).reshape((NX, NY, NZ, D))
    return lax.map(one_sample, tokens)
```

```python
import functools
import jax
import jax.numpy as jnp
from jax import lax
from jax.experimental import pallas as pl
from jax.experimental.pallas import tpu as pltpu
from jax.sharding import Mesh
from jax.sharding import PartitionSpec as P

HEADS = 16
HEAD = 64
PAIRS = HEADS // 2
BLOCK = 128
NEG = -1e30
DIMS = (2, 16, 2, 4, 2)
ALL = ("yh", "z", "yl", "x", "c")
GY = ("yh", "z")
GZ = ("yl", "x", "c")
BF = jnp.bfloat16
F32 = jnp.float32


def index_of(yh, z, yl, x, c):
    return (((yh * DIMS[1] + z) * DIMS[2] + yl) * DIMS[3] + x) * DIMS[4] + c


def every_device():
    for yh in range(DIMS[0]):
        for z in range(DIMS[1]):
            for yl in range(DIMS[2]):
                for x in range(DIMS[3]):
                    for c in range(DIMS[4]):
                        yield yh, z, yl, x, c


def step_x():
    return [
        (index_of(*d), index_of(d[0], d[1], d[2], (d[3] + (1 - 2 * d[4])) % DIMS[3], d[4]))
        for d in every_device()
    ]


def step_y():
    pairs = []
    for yh, z, yl, x, c in every_device():
        y = (yh * 2 + yl + (1 - 2 * c)) % 4
        pairs.append((index_of(yh, z, yl, x, c), index_of(y // 2, z, y % 2, x, c)))
    return pairs


def iota(shape, dim):
    return lax.broadcasted_iota(jnp.int32, shape, dim)


def line_rows(axis, i):
    if axis == 1:
        return (i // 128) * 128 + (i % 64) * 2 + (i // 64) % 2
    if axis == 2:
        return (i % 32) * 8 + i // 32
    return ((i % 32) // 2) * 16 + (i // 32) * 2 + i % 2


def norm_kernel(tokens_ref, out_ref):
    values = tokens_ref[...].astype(F32)
    center = jnp.mean(values, axis=-1, keepdims=True)
    values = values - center
    spread = jnp.mean(values * values, axis=-1, keepdims=True)
    out_ref[...] = (values * lax.rsqrt(spread + 1e-05)).astype(BF)


def bias_kernel(length, table_ref, out_ref):
    lanes = iota((length, BLOCK), 1) // length
    for head in range(HEADS):
        row = jnp.broadcast_to(table_ref[head : head + 1, :], (length, BLOCK))
        for place in range(BLOCK // length):
            shift = (place * length - length + 1) % BLOCK
            turned = pltpu.roll(row, shift, 1, stride=1, stride_axis=0)
            out_ref[
                head // 2,
                place * length : (place + 1) * length,
                (head % 2) * BLOCK : (head % 2 + 1) * BLOCK,
            ] = jnp.where(lanes == place, turned, NEG)


def attend_kernel(axis, groups, pair_ref, tokens_ref, *refs):
    weight_refs = refs[: 2 * groups]
    bias_ref, out_ref, lines_ref = refs[2 * groups :]
    step = pl.program_id(0)
    rows = tokens_ref.shape[0]
    order = line_rows(axis, iota((rows, rows), 0)) == iota((rows, rows), 1)

    @pl.when(step == 0)
    def _():
        turn = order.astype(F32).astype(BF)
        lines_ref[...] = jnp.dot(turn, tokens_ref[...], preferred_element_type=F32).astype(BF)

    own, other = weight_refs[0][0], weight_refs[1][0]
    if groups == 2:
        first = step < 4
        own = jnp.where(first, own, weight_refs[2][0])
        other = jnp.where(first, other, weight_refs[3][0])
    core = pair_ref[pair_ref.shape[0] - 1]
    low = jnp.where(core == 0, own, other)
    high = jnp.where(core == 0, other, own)
    depth, width = low.shape
    weights = jnp.stack(
        [low.reshape(depth // 16, 16, width), high.reshape(depth // 16, 16, width)], axis=1
    ).reshape(2 * depth, width)
    qkv = jnp.dot(lines_ref[...], weights, preferred_element_type=F32).astype(BF)
    left = iota((BLOCK, BLOCK), 1) < HEAD
    zero = jnp.zeros((BLOCK, BLOCK), BF)
    mixed = []
    for start in range(0, rows, BLOCK):
        part = qkv[start : start + BLOCK]
        q, k, v = part[:, :BLOCK], part[:, BLOCK : 2 * BLOCK], part[:, 2 * BLOCK :]
        keys = jnp.concatenate([jnp.where(left, k, zero), jnp.where(left, zero, k)], axis=0)
        values = jnp.concatenate([jnp.where(left, v, zero), jnp.where(left, zero, v)], axis=0)
        scores = lax.dot_general(q, keys, (((1,), (1,)), ((), ())), preferred_element_type=F32)
        scores = scores * HEAD ** (-0.5) + bias_ref[0]
        probs = []
        for half in range(2):
            s = scores[:, half * BLOCK : (half + 1) * BLOCK]
            e = jnp.exp(s - jnp.max(s, axis=-1, keepdims=True))
            probs.append((e / jnp.sum(e, axis=-1, keepdims=True)).astype(BF))
        probs = jnp.concatenate(probs, axis=1)
        mixed.append(jnp.dot(probs, values, preferred_element_type=F32).astype(BF))
    mixed = jnp.concatenate(mixed, axis=0)
    back = (line_rows(axis, iota((rows, rows), 1)) == iota((rows, rows), 0)).astype(F32).astype(BF)
    out_ref[...] = jnp.dot(back, mixed, preferred_element_type=F32).astype(BF)


def attend(axis, tokens, weights, bias, pairs, columns, core):
    groups = len(weights) // 2
    steps = 4 * groups
    rows, features = tokens.shape
    half, width = weights[0].shape[1:]
    specs = [pl.BlockSpec((rows, features), lambda s, p: (0, 0))]
    for group in range(groups):

        def own_slot(s, p, group=group):
            return (jnp.clip(s - 4 * group, 0, 3), 0, 0)

        def other_slot(s, p, group=group):
            return ((4 - jnp.clip(s - 4 * group, 0, 3)) % 4, 0, 0)

        specs.append(pl.BlockSpec((1, half, width), own_slot))
        specs.append(pl.BlockSpec((1, half, width), other_slot))
    specs.append(pl.BlockSpec((1, BLOCK, 2 * BLOCK), lambda s, p: (p[s], 0, 0)))
    scalars = jnp.concatenate([pairs, columns, core[None]]).astype(jnp.int32)
    return pl.pallas_call(
        functools.partial(attend_kernel, axis, groups),
        out_shape=jax.ShapeDtypeStruct((rows, steps * BLOCK), BF),
        grid_spec=pltpu.PrefetchScalarGridSpec(
            num_scalar_prefetch=1,
            grid=(steps,),
            in_specs=specs,
            out_specs=pl.BlockSpec((rows, BLOCK), lambda s, p: (0, p[steps + s])),
            scratch_shapes=[pltpu.VMEM((rows, features), BF)],
        ),
        compiler_params=pltpu.CompilerParams(vmem_limit_bytes=40 * 2**20),
        cost_estimate=pl.CostEstimate(
            flops=2 * rows * features * 3 * BLOCK * steps,
            bytes_accessed=steps * 1024 * 1024,
            transcendentals=steps * rows * 2 * BLOCK,
        ),
        name=f"attend_{axis}_{groups}",
    )(scalars, tokens, *weights, bias)


def final_kernel(side_ref, tokens_ref, x_ref, ya_ref, yb_ref, z_ref, w_ref, out_ref):
    side = side_ref[0]
    ya, yb = ya_ref[...], yb_ref[...]
    y = jnp.concatenate([jnp.where(side == 0, ya, yb), jnp.where(side == 0, yb, ya)], axis=1)
    summed = x_ref[...].astype(F32) + y.astype(F32) + z_ref[...].astype(F32)
    result = jnp.dot(summed.astype(BF), w_ref[...], preferred_element_type=F32)
    out_ref[...] = (tokens_ref[...].astype(F32) + result).astype(BF)


def whole(kernel, out, name, scalars=0):
    vmem = pl.BlockSpec(memory_space=pltpu.VMEM)
    smem = pl.BlockSpec(memory_space=pltpu.SMEM)

    def call(*args):
        return pl.pallas_call(
            kernel,
            out_shape=out,
            in_specs=[smem] * scalars + [vmem] * (len(args) - scalars),
            out_specs=vmem,
            compiler_params=pltpu.CompilerParams(vmem_limit_bytes=40 * 2**20),
            name=name,
        )(*args)

    return call


def reversed_table(table):
    turned = table[:, ::-1]
    return jnp.pad(turned, ((0, 0), (0, BLOCK - turned.shape[1])))


def bias_blocks(table):
    length = (table.shape[1] + 1) // 2
    shape = jax.ShapeDtypeStruct((PAIRS, BLOCK, 2 * BLOCK), F32)
    return whole(functools.partial(bias_kernel, length), shape, f"bias_{length}")(
        reversed_table(table)
    )


def exchange(array, axes):
    return lax.all_to_all(array, axes, split_axis=0, concat_axis=0, tiled=True)


def swap_cores(array):
    return lax.ppermute(array, "c", [(0, 1), (1, 0)])


def shards(tokens, w_qkv, w_out, bias_x, bias_y, bias_z):
    features = tokens.shape[-1]
    shape = tokens.shape
    yl, x, c = lax.axis_index("yl"), lax.axis_index("x"), lax.axis_index("c")
    pair = yl * DIMS[3] + x

    depth = w_qkv.shape[0] // 2
    mine = jnp.concatenate(
        [
            lax.dynamic_slice(w_qkv, (c * depth, part * features + pair * BLOCK), (depth, BLOCK))
            for part in range(3)
        ],
        axis=1,
    )
    peers = DIMS[0] * DIMS[1]
    piece = exchange(jnp.broadcast_to(mine[None], (peers, *mine.shape)), GY)
    piece = piece.reshape(peers * depth, 3 * BLOCK)

    flat = tokens.reshape(-1, features)
    rows = flat.shape[0]
    normed = whole(norm_kernel, jax.ShapeDtypeStruct(flat.shape, BF), "norm")(flat)
    y_lines = exchange(normed.reshape(peers, -1, features), GY).reshape(rows, features)
    zs = DIMS[2] * DIMS[3] * DIMS[4]
    z_lines = exchange(normed.reshape(zs, -1, features), GZ).reshape(rows, features)

    around_x = functools.partial(lax.ppermute, axis_name=ALL, perm=step_x())
    around_y = functools.partial(lax.ppermute, axis_name=ALL, perm=step_y())
    held = [piece]
    for _ in range(DIMS[3] - 1):
        held.append(around_x(held[-1]))
    across = [around_y(p) for p in held]
    own_a = jnp.stack(held)
    own_b = jnp.stack(across)
    other_a = swap_cores(own_a)
    other_b = swap_cores(own_b)

    columns = (x - jnp.arange(4) * (1 - 2 * c)) % DIMS[3]
    pairs_a = yl * 4 + columns
    pairs_b = (1 - yl) * 4 + columns
    pairs = jnp.concatenate([pairs_a, pairs_b])

    blocks_x = bias_blocks(bias_x)
    blocks_y = bias_blocks(bias_y)
    blocks_z = bias_blocks(bias_z)

    w_half = lax.dynamic_slice(
        w_out, (0, c * (features // 2)), (w_out.shape[0], features // 2)
    )
    w_half = lax.all_gather(w_half, "z", axis=0, tiled=True)
    w_half = lax.all_gather(w_half, "yh", axis=0, tiled=True)
    w_other = swap_cores(w_half)
    w_full = jnp.concatenate(
        [jnp.where(c == 0, w_half, w_other), jnp.where(c == 0, w_other, w_half)], axis=1
    )

    y_a = attend(2, y_lines, (own_a, other_a), blocks_y, pairs_a, columns, c)
    y_a = exchange(y_a.reshape(peers, -1, features // 2), GY).reshape(rows, -1)
    y_b = attend(2, y_lines, (own_b, other_b), blocks_y, pairs_b, columns, c)
    y_b = exchange(y_b.reshape(peers, -1, features // 2), GY).reshape(rows, -1)
    every = (own_a, other_a, own_b, other_b)
    z = attend(3, z_lines, every, blocks_z, pairs, pairs, c)
    z = exchange(z.reshape(zs, -1, features), GZ).reshape(rows, features)
    along_x = attend(1, normed, every, blocks_x, pairs, pairs, c)
    mixed = whole(final_kernel, jax.ShapeDtypeStruct(flat.shape, BF), "mix", 1)(
        yl[None], flat, along_x, y_a, y_b, z, w_full
    )
    return mixed.reshape(shape)


def solution(mesh):
    torus = Mesh(mesh.devices.reshape(DIMS), ALL)
    in_specs = (P(None, None, GY, GZ, None), P(GY, None), P(GY, None), P(), P(), P())
    return jax.shard_map(
        shards, mesh=torus, in_specs=in_specs, out_specs=in_specs[0], check_vma=False
    )
```

```python
import functools
import jax
import jax.numpy as jnp
from jax import lax
from jax.experimental import pallas as pl
from jax.experimental.pallas import tpu as pltpu
from jax.sharding import Mesh
from jax.sharding import PartitionSpec as P

HEADS = 16
HEAD = 64
PAIRS = HEADS // 2
BLOCK = 128
NEG = -1e30
DIMS = (2, 16, 2, 4, 2)
ALL = ("yh", "z", "yl", "x", "c")
GY = ("yh", "z")
GZ = ("yl", "x", "c")
BF = jnp.bfloat16
F32 = jnp.float32


def index_of(yh, z, yl, x, c):
    return (((yh * DIMS[1] + z) * DIMS[2] + yl) * DIMS[3] + x) * DIMS[4] + c


def every_device():
    for yh in range(DIMS[0]):
        for z in range(DIMS[1]):
            for yl in range(DIMS[2]):
                for x in range(DIMS[3]):
                    for c in range(DIMS[4]):
                        yield yh, z, yl, x, c


def hop_x(far):
    return [
        (index_of(*d), index_of(d[0], d[1], d[2], (d[3] + far) % DIMS[3], d[4]))
        for d in every_device()
    ]


def hop_y(far):
    pairs = []
    for yh, z, yl, x, c in every_device():
        y = (yh * 2 + yl + far) % 4
        pairs.append((index_of(yh, z, yl, x, c), index_of(y // 2, z, y % 2, x, c)))
    return pairs


def iota(shape, dim):
    return lax.broadcasted_iota(jnp.int32, shape, dim)


def line_rows(axis, i):
    if axis == 1:
        return (i & 128) + (i & 63) * 2 + ((i >> 6) & 1)
    if axis == 2:
        return (i & 31) * 8 + (i >> 5)
    return ((i & 30) << 3) + ((i >> 5) << 1) + (i & 1)


def norm_kernel(tokens_ref, out_ref):
    values = tokens_ref[...].astype(F32)
    center = jnp.mean(values, axis=-1, keepdims=True)
    values = values - center
    spread = jnp.mean(values * values, axis=-1, keepdims=True)
    out_ref[...] = (values * lax.rsqrt(spread + 1e-05)).astype(BF)


def bias_kernel(length, table_ref, out_ref):
    lanes = iota((length, BLOCK), 1) // length
    for head in range(HEADS):
        row = jnp.broadcast_to(table_ref[head : head + 1, :], (length, BLOCK))
        for place in range(BLOCK // length):
            shift = (place * length - length + 1) % BLOCK
            turned = pltpu.roll(row, shift, 1, stride=1, stride_axis=0)
            out_ref[
                head // 2,
                place * length : (place + 1) * length,
                (head % 2) * BLOCK : (head % 2 + 1) * BLOCK,
            ] = jnp.where(lanes == place, turned, NEG)


def interleaved(own, other, core):
    depth, width = own.shape
    low = jnp.where(core == 0, own, other).reshape(depth // 16, 16, width)
    high = jnp.where(core == 0, other, own).reshape(depth // 16, 16, width)
    return jnp.stack([low, high], axis=1).reshape(2 * depth, width)


def assembled(parts, turned, core):
    halves = [interleaved(own, other, core) for own, other in parts]
    low = jnp.where(turned == 0, halves[0], halves[1])
    high = jnp.where(turned == 0, halves[1], halves[0])
    return jnp.concatenate([low, high], axis=0)


def attend_kernel(axis, scalar_ref, tokens_ref, *refs):
    weight_refs, bias_refs = refs[:4], refs[4:6]
    out_ref, lines_ref, back_ref, qkv_ref, mixed_ref = refs[-5:]
    step = pl.program_id(0)
    rows = tokens_ref.shape[0]
    core, turned_a, turned_b, yl, x = [scalar_ref[8 + n] for n in range(5)]

    @pl.when(step == 0)
    def _():
        turn = line_rows(axis, iota((rows, 1), 0)) == iota((rows, rows), 1)
        turn = turn.astype(F32).astype(BF)
        lines_ref[...] = jnp.dot(turn, tokens_ref[...], preferred_element_type=F32).astype(BF)
        place = iota((rows, 1), 0)
        if axis == 3:
            dx, dy, dc = place >> 6, (place >> 5) & 1, (place >> 4) & 1
            to = (yl ^ dy) * 8 + ((x + dx) & 3) * 2 + (core ^ dc)
            back = ((place >> 1) & 7) * 32 + to * 2 + (place & 1) == iota((rows, rows), 1)
        else:
            back = line_rows(axis, iota((1, rows), 1)) == iota((rows, rows), 0)
        back_ref[...] = back.astype(F32).astype(BF)

    width = 3 * BLOCK
    left = iota((BLOCK, BLOCK), 1) < HEAD
    zero = jnp.zeros((BLOCK, BLOCK), BF)
    projected = (step + 1) % 2
    for n in range(2):
        mixed = []
        for start in range(0, rows, BLOCK):
            q, k, v = [
                qkv_ref[projected, start : start + BLOCK, n * width + m * BLOCK : n * width + (m + 1) * BLOCK]
                for m in range(3)
            ]
            keys = jnp.concatenate([jnp.where(left, k, zero), jnp.where(left, zero, k)], axis=0)
            values = jnp.concatenate([jnp.where(left, v, zero), jnp.where(left, zero, v)], axis=0)
            scores = lax.dot_general(q, keys, (((1,), (1,)), ((), ())), preferred_element_type=F32)
            scores = scores * HEAD ** (-0.5) + bias_refs[n][0]
            probs = []
            for half in range(2):
                s = scores[:, half * BLOCK : (half + 1) * BLOCK]
                e = jnp.exp(s - jnp.max(s, axis=-1, keepdims=True))
                probs.append((e * (1.0 / jnp.sum(e, axis=-1, keepdims=True))).astype(BF))
            probs = jnp.concatenate(probs, axis=1)
            mixed.append(jnp.dot(probs, values, preferred_element_type=F32).astype(BF))
        pair = scalar_ref[2 * jnp.maximum(step - 1, 0) + n]
        columns = pl.ds(pl.multiple_of(pair * BLOCK, BLOCK), BLOCK)
        mixed_ref[:, columns] = jnp.concatenate(mixed, axis=0)

    turned = jnp.where(step < 2, turned_a, turned_b)
    near_own, near_other, far_own, far_other = weight_refs
    weights = []
    for n in range(2):
        parts = [
            (
                jnp.concatenate([near_own[0, m, n], far_own[n, 0, m]], axis=0),
                jnp.concatenate([near_other[0, m, n], far_other[n, 0, m]], axis=0),
            )
            for m in range(2)
        ]
        weights.append(assembled(parts, turned, core))
    weights = jnp.concatenate(weights, axis=1)
    qkv = jnp.dot(lines_ref[...], weights, preferred_element_type=F32)
    qkv_ref[step % 2] = qkv.astype(BF)

    @pl.when(step == pl.num_programs(0) - 1)
    def _():
        out_ref[...] = jnp.dot(
            back_ref[...], mixed_ref[...], preferred_element_type=F32
        ).astype(BF)


def attend(axis, tokens, weights, bias, scalars, after=()):
    rows, features = tokens.shape
    half, width = weights[0].shape[3:]
    specs = [pl.BlockSpec((rows, features), lambda s, p: (0, 0))]

    def near(s, p):
        s = jnp.minimum(s, 3)
        return (s // 2, 0, s % 2, 0, 0)

    def far(s, p):
        s = jnp.minimum(s, 3)
        return (s % 2, s // 2, 0, 0, 0)

    specs.extend([pl.BlockSpec((1, 2, 2, half, width), near)] * 2)
    specs.extend([pl.BlockSpec((2, 1, 2, half, width), far)] * 2)
    for n in range(2):

        def pair(s, p, n=n):
            return (p[2 * jnp.maximum(s - 1, 0) + n], 0, 0)

        specs.append(pl.BlockSpec((1, BLOCK, 2 * BLOCK), pair))
    specs.extend([pl.BlockSpec(memory_space=pl.ANY)] * len(after))
    return pl.pallas_call(
        functools.partial(attend_kernel, axis),
        out_shape=jax.ShapeDtypeStruct((rows, HEADS * HEAD), BF),
        grid_spec=pltpu.PrefetchScalarGridSpec(
            num_scalar_prefetch=1,
            grid=(5,),
            in_specs=specs,
            out_specs=pl.BlockSpec((rows, features), lambda s, p: (0, 0)),
            scratch_shapes=[
                pltpu.VMEM((rows, features), BF),
                pltpu.VMEM((rows, rows), BF),
                pltpu.VMEM((2, rows, 2 * width), BF),
                pltpu.VMEM((rows, features), BF),
            ],
        ),
        compiler_params=pltpu.CompilerParams(vmem_limit_bytes=61 * 2**20),
        cost_estimate=pl.CostEstimate(flops=1000, bytes_accessed=1000, transcendentals=0),
        name=f"attend_{axis}",
    )(scalars, tokens, *weights, bias, bias, *after)


def mix_kernel(scalar_ref, tokens_ref, x_ref, y_ref, z0, z1, z2, z3, zy_ref, zc_ref, own_ref, other_ref, out_ref, z_ref):
    core, yl, x = scalar_ref[8], scalar_ref[11], scalar_ref[12]
    for k, ref in enumerate((z0, z1, z2, z3)):
        for dy in range(2):
            for dc in range(2):
                if dc == 1:
                    rows = zc_ref[dy * 4 + k]
                elif dy == 1:
                    rows = zy_ref[k, :16]
                else:
                    rows = ref[:16]
                source = (yl ^ dy) * 8 + ((x - k + 4) % 4) * 2 + (core ^ dc)
                z_ref[pl.ds(pl.multiple_of(source * 16, 16), 16), :] = rows
    summed = x_ref[...].astype(F32) + y_ref[...].astype(F32) + z_ref[...].astype(F32)
    summed = summed.astype(BF)
    for pair in range(PAIRS):
        weights = jnp.concatenate(
            [interleaved(own_ref[h, pair], other_ref[h, pair], core) for h in range(2)], axis=0
        )
        columns = slice(pair * BLOCK, (pair + 1) * BLOCK)
        result = jnp.dot(summed, weights, preferred_element_type=F32)
        out_ref[:, columns] = (tokens_ref[:, columns].astype(F32) + result).astype(BF)


def whole(kernel, out, name, scalars=0, scratch=()):
    vmem = pl.BlockSpec(memory_space=pltpu.VMEM)
    smem = pl.BlockSpec(memory_space=pltpu.SMEM)

    def call(*args):
        return pl.pallas_call(
            kernel,
            out_shape=out,
            in_specs=[smem] * scalars + [vmem] * (len(args) - scalars),
            out_specs=vmem,
            scratch_shapes=list(scratch),
            compiler_params=pltpu.CompilerParams(vmem_limit_bytes=61 * 2**20),
            name=name,
        )(*args)

    return call


def reversed_table(table):
    turned = table[:, ::-1]
    return jnp.pad(turned, ((0, 0), (0, BLOCK - turned.shape[1])))


def bias_blocks(table):
    length = (table.shape[1] + 1) // 2
    shape = jax.ShapeDtypeStruct((PAIRS, BLOCK, 2 * BLOCK), F32)
    return whole(functools.partial(bias_kernel, length), shape, f"bias_{length}")(
        reversed_table(table)
    )


def exchange(array, axes):
    return lax.all_to_all(array, axes, split_axis=0, concat_axis=0, tiled=True)


def swap(array, axis):
    return lax.ppermute(array, axis, [(0, 1), (1, 0)])


def together(array, other):
    return lax.optimization_barrier((array, other))[0]


def shards(tokens, w_qkv, w_out, bias_x, bias_y, bias_z):
    features = tokens.shape[-1]
    shape = tokens.shape
    yh, yl = lax.axis_index("yh"), lax.axis_index("yl")
    x, c = lax.axis_index("x"), lax.axis_index("c")
    pair = yl * DIMS[3] + x
    peers = DIMS[0] * DIMS[1]
    zs = DIMS[2] * DIMS[3] * DIMS[4]

    depth = w_qkv.shape[0] // 2
    mine = [
        lax.dynamic_slice(w_qkv, (c * depth, part * features + pair * BLOCK), (depth, BLOCK))
        for part in range(3)
    ]
    mine.append(lax.dynamic_slice(w_out, (c * depth, pair * BLOCK), (depth, BLOCK)))
    mine = jnp.concatenate(mine, axis=1)
    piece = exchange(jnp.broadcast_to(mine[None], (DIMS[1], *mine.shape)), "z")
    piece = piece.reshape(DIMS[1] * depth, 4 * BLOCK)
    flat = tokens.reshape(-1, features)
    rows = flat.shape[0]
    normed = whole(norm_kernel, jax.ShapeDtypeStruct(flat.shape, BF), "norm")(flat)
    blocks_x = bias_blocks(bias_x)
    blocks_y = bias_blocks(bias_y)
    blocks_z = bias_blocks(bias_z)
    piece = together(piece, (normed, blocks_x, blocks_y, blocks_z))
    out_piece = piece[:, 3 * BLOCK :]
    piece = piece[:, : 3 * BLOCK]

    y_lines = exchange(normed.reshape(peers, -1, features), GY).reshape(rows, features)
    z_lines = exchange(together(normed, y_lines).reshape(zs, -1, features), GZ)
    z_lines = z_lines.reshape(rows, features)

    tall = piece.shape[0] // 2
    along = [piece[:tall]] + [lax.ppermute(piece[:tall], ALL, hop_x(k)) for k in range(1, 4)]
    across = [piece[tall:]] + [lax.ppermute(piece[tall:], ALL, hop_y(m)) for m in range(1, 4)]
    along = jnp.stack(along)
    across = jnp.stack([across[m] for m in (0, 2, 1, 3)])
    near = [along] + [lax.ppermute(along, ALL, hop_y(m)) for m in range(1, 4)]
    far = [across] + [lax.ppermute(across, ALL, hop_x(k)) for k in range(1, 4)]
    near = jnp.stack([near[m] for m in (0, 2, 1, 3)]).reshape(2, 2, *along.shape)
    far = jnp.stack(far).reshape(4, 2, 2, *piece[:tall].shape)
    near_other = swap(near, "c")
    far_other = swap(far, "c")

    out_own = lax.all_gather(out_piece, ("yh", "yl", "x"), axis=0, tiled=True)
    out_own = out_own.reshape(2, PAIRS, -1, BLOCK)

    columns = (x - jnp.arange(4)) % DIMS[3]
    y = yh * 2 + yl
    turned_b = ((y - 1) % 4) // 2
    scalars = jnp.concatenate(
        [yl * 4 + columns, (1 - yl) * 4 + columns, jnp.stack([c, yh, turned_b, yl, x])]
    ).astype(jnp.int32)

    every = (near, near_other, far, far_other)
    along_y = attend(2, y_lines, every, blocks_y, scalars)
    z = attend(3, z_lines, every, blocks_z, scalars, (along_y,))
    along_y = exchange(together(along_y, z_lines).reshape(peers, -1, features), GY).reshape(rows, features)
    along_x = attend(1, normed, every, blocks_x, scalars, (z,))

    out_own = together(out_own, along_x)
    out_other = swap(out_own, "c")
    z = z.reshape(4, rows // 4, features)
    back = [z[0]] + [lax.ppermute(z[k], ALL, hop_x(k)) for k in range(1, 4)]
    back_y = swap(together(jnp.stack([b[32:] for b in back]), along_x), "yl")
    back_c = jnp.stack([b[16:32] for b in back] + [back_y[k, 16:] for k in range(4)])
    back_c = swap(together(back_c, along_y), "c")
    mixed = whole(
        mix_kernel, jax.ShapeDtypeStruct(flat.shape, BF), "mix", 1, [pltpu.VMEM(flat.shape, BF)]
    )(scalars, flat, along_x, along_y, *back, back_y, back_c, out_own, out_other)
    return mixed.reshape(shape)


def solution(mesh):
    torus = Mesh(mesh.devices.reshape(DIMS), ALL)
    in_specs = (P(None, None, GY, GZ, None), P(GY, None), P(GY, None), P(), P(), P())
    return jax.shard_map(
        shards, mesh=torus, in_specs=in_specs, out_specs=in_specs[0], check_vma=False
    )
```

```python
import functools
import jax
import jax.numpy as jnp
from jax import lax
from jax.experimental import pallas as pl
from jax.experimental.pallas import tpu as pltpu
from jax.sharding import Mesh
from jax.sharding import PartitionSpec as P

HEADS = 16
HEAD = 64
PAIRS = HEADS // 2
BLOCK = 128
NEG = -1e30
HOPS = (0, 2, 1, 3)
DIMS = (2, 16, 2, 4, 2)
ALL = ("yh", "z", "yl", "x", "c")
GY = ("yh", "z")
GZ = ("yl", "x", "c")
BF = jnp.bfloat16
F32 = jnp.float32


def index_of(yh, z, yl, x, c):
    return (((yh * DIMS[1] + z) * DIMS[2] + yl) * DIMS[3] + x) * DIMS[4] + c


def every_device():
    for yh in range(DIMS[0]):
        for z in range(DIMS[1]):
            for yl in range(DIMS[2]):
                for x in range(DIMS[3]):
                    for c in range(DIMS[4]):
                        yield yh, z, yl, x, c


def hop_x(far):
    return [
        (index_of(*d), index_of(d[0], d[1], d[2], (d[3] + far) % DIMS[3], d[4]))
        for d in every_device()
    ]


def hop_plane(far, x_core):
    pairs = []
    for yh, z, yl, x, c in every_device():
        y = yh * 2 + yl
        if c == x_core:
            x_to, y_to = (x + far) % 4, y
        else:
            x_to, y_to = x, (y + far) % 4
        pairs.append((index_of(yh, z, yl, x, c), index_of(y_to // 2, z, y_to % 2, x_to, c)))
    return pairs


def iota(shape, dim):
    return lax.broadcasted_iota(jnp.int32, shape, dim)


def line_rows(axis, i):
    if axis == 1:
        return (i & 128) + (i & 63) * 2 + ((i >> 6) & 1)
    if axis == 2:
        return (i & 31) * 8 + (i >> 5)
    return ((i & 30) << 3) + ((i >> 5) << 1) + (i & 1)


def norm_kernel(tokens_ref, out_ref):
    values = tokens_ref[...].astype(F32)
    center = jnp.mean(values, axis=-1, keepdims=True)
    values = values - center
    spread = jnp.mean(values * values, axis=-1, keepdims=True)
    out_ref[...] = (values * lax.rsqrt(spread + 1e-05)).astype(BF)


def bias_kernel(length, table_ref, out_ref):
    lanes = iota((length, BLOCK), 1) // length
    for head in range(HEADS):
        row = jnp.broadcast_to(table_ref[head : head + 1, :], (length, BLOCK))
        for place in range(BLOCK // length):
            shift = (place * length - length + 1) % BLOCK
            turned = pltpu.roll(row, shift, 1, stride=1, stride_axis=0)
            out_ref[
                head // 2,
                place * length : (place + 1) * length,
                (head % 2) * BLOCK : (head % 2 + 1) * BLOCK,
            ] = jnp.where(lanes == place, turned, NEG)


def attend_kernel(axes, scalar_ref, *refs):
    count = len(axes)
    token_refs, refs = refs[:count], refs[count:]
    weight_refs, refs = refs[:8], refs[8:]
    bias_refs = refs[: 2 * count]
    refs = refs[-(count * 2 + 3) :]
    out_refs, back_refs = refs[:count], refs[count : 2 * count]
    lines_ref, qkv_ref, mixed_ref = refs[2 * count :]
    step = pl.program_id(0)
    rows = token_refs[0].shape[0]
    core, turned_a, turned_b, yl, x = [scalar_ref[8 + n] for n in range(5)]

    @pl.when(step == 0)
    def _():
        for a, axis in enumerate(axes):
            turn = line_rows(axis, iota((rows, 1), 0)) == iota((rows, rows), 1)
            turn = turn.astype(F32).astype(BF)
            lines = jnp.dot(turn, token_refs[a][...], preferred_element_type=F32)
            lines_ref[a * rows : (a + 1) * rows] = lines.astype(BF)
            place = iota((rows, 1), 0)
            if axis == 3:
                dx, dy, dc = place >> 6, (place >> 5) & 1, (place >> 4) & 1
                to = (yl ^ dy) * 8 + ((x + dx) & 3) * 2 + (core ^ dc)
                back = ((place >> 1) & 7) * 32 + to * 2 + (place & 1) == iota((rows, rows), 1)
            else:
                back = line_rows(axis, iota((1, rows), 1)) == iota((rows, rows), 0)
            back_refs[a][...] = back.astype(F32).astype(BF)

    width = 3 * BLOCK

    def attention():
        left = iota((BLOCK, BLOCK), 1) < HEAD
        zero = jnp.zeros((BLOCK, BLOCK), BF)
        projected = (step + 1) % 2
        for n in range(2):
            pair = scalar_ref[2 * jnp.maximum(step - 1, 0) + n]
            columns = pl.ds(pl.multiple_of(pair * BLOCK, BLOCK), BLOCK)
            for start in range(0, count * rows, BLOCK):
                q, k, v = [
                    qkv_ref[
                        projected,
                        start : start + BLOCK,
                        n * width + m * BLOCK : n * width + (m + 1) * BLOCK,
                    ]
                    for m in range(3)
                ]
                keys = jnp.concatenate([jnp.where(left, k, zero), jnp.where(left, zero, k)], axis=0)
                values = jnp.concatenate([jnp.where(left, v, zero), jnp.where(left, zero, v)], axis=0)
                scores = lax.dot_general(q, keys, (((1,), (1,)), ((), ())), preferred_element_type=F32)
                scores = scores * HEAD ** (-0.5) + bias_refs[2 * (start // rows) + n][0]
                probs = []
                for half in range(2):
                    s = scores[:, half * BLOCK : (half + 1) * BLOCK]
                    e = jnp.exp(s - jnp.max(s, axis=-1, keepdims=True))
                    probs.append((e * (1.0 / jnp.sum(e, axis=-1, keepdims=True))).astype(BF))
                probs = jnp.concatenate(probs, axis=1)
                mixed = jnp.dot(probs, values, preferred_element_type=F32).astype(BF)
                mixed_ref[start : start + BLOCK, columns] = mixed

    def projection():
        turned = jnp.where(step < 2, turned_a, turned_b)
        near_first, far_first = step < 2, step % 2 == 0
        own_first = jnp.where(core == 0, near_first, far_first)
        other_first = jnp.where(core == 0, far_first, near_first)
        own_refs, other_refs = weight_refs[:4], weight_refs[4:]
        weights = []
        for n in range(2):
            halves = []
            for m in range(2):
                own, other = [
                    [jnp.where(early, part[2 * i][j], part[2 * i + 1][j]) for i, j in ((m, n), (n, m))]
                    for part, early in ((own_refs, own_first), (other_refs, other_first))
                ]
                near = jnp.where(core == 0, own[0], other[0])
                far = jnp.where(core == 0, other[1], own[1])
                halves.append(jnp.concatenate([near, far], axis=0))
            low = jnp.where(turned == 0, halves[0], halves[1])
            high = jnp.where(turned == 0, halves[1], halves[0])
            weights.append(jnp.concatenate([low, high], axis=0))
        weights = jnp.concatenate(weights, axis=1)
        qkv = jnp.dot(lines_ref[...], weights, preferred_element_type=F32)
        qkv_ref[step % 2] = qkv.astype(BF)

    last = pl.num_programs(0) - 1

    @pl.when(step == 0)
    def _():
        projection()

    @pl.when(jnp.logical_and(step > 0, step < last))
    def _():
        attention()
        projection()

    @pl.when(step == last)
    def _():
        attention()
        for a in range(count):
            mixed = mixed_ref[a * rows : (a + 1) * rows]
            out = jnp.dot(back_refs[a][...], mixed, preferred_element_type=F32)
            out_refs[a][...] = out.astype(BF)


def attend(axes, tokens, weights, biases, scalars, after=()):
    rows, features = tokens[0].shape
    half, width = weights[0].shape[1], 3 * BLOCK
    count = len(axes)
    specs = [pl.BlockSpec((rows, features), lambda s, p: (0, 0))] * count

    for other in range(2):
        for hop in range(4):
            late = hop % 2

            def block(s, p, other=other, late=late):
                s = jnp.minimum(s, 3)
                y_part, x_part = s // 2, s % 2
                near = jnp.where(y_part == late, x_part, 1 - late)
                return (jnp.where(p[8] == other, near, y_part), 0, 0)

            specs.append(pl.BlockSpec((2, half, width), block))
    for _ in range(count):
        for n in range(2):

            def pair(s, p, n=n):
                return (p[2 * jnp.maximum(s - 1, 0) + n], 0, 0)

            specs.append(pl.BlockSpec((1, BLOCK, 2 * BLOCK), pair))
    specs.extend([pl.BlockSpec(memory_space=pl.ANY)] * len(after))
    bias_args = [b for bias in biases for b in (bias, bias)]
    return pl.pallas_call(
        functools.partial(attend_kernel, axes),
        out_shape=[jax.ShapeDtypeStruct((rows, HEADS * HEAD), BF)] * count,
        grid_spec=pltpu.PrefetchScalarGridSpec(
            num_scalar_prefetch=1,
            grid=(5,),
            in_specs=specs,
            out_specs=[pl.BlockSpec((rows, features), lambda s, p: (0, 0))] * count,
            scratch_shapes=[pltpu.VMEM((rows, rows), BF)] * count
            + [
                pltpu.VMEM((count * rows, features), BF),
                pltpu.VMEM((2, count * rows, 2 * width), BF),
                pltpu.VMEM((count * rows, features), BF),
            ],
        ),
        compiler_params=pltpu.CompilerParams(vmem_limit_bytes=61 * 2**20),
        cost_estimate=pl.CostEstimate(flops=1000, bytes_accessed=1000, transcendentals=0),
        name="attend_" + "_".join(map(str, axes)),
    )(scalars, *tokens, *weights, *bias_args, *after)


def mix_kernel(scalar_ref, tokens_ref, x_ref, y_ref, z0, z1, z2, z3, zy_ref, zc_ref, *refs):
    own_refs, other_refs, (out_ref, z_ref) = refs[:4], refs[4:8], refs[8:]
    core, turned_a, turned_b, yl, x = [scalar_ref[8 + n] for n in range(5)]
    for k, ref in enumerate((z0, z1, z2, z3)):
        for dy in range(2):
            for dc in range(2):
                if dy == 1:
                    rows = zy_ref[dc * 4 + k]
                elif dc == 1:
                    rows = zc_ref[k]
                else:
                    rows = ref[:16]
                source = (yl ^ dy) * 8 + ((x - k + 4) % 4) * 2 + (core ^ dc)
                z_ref[pl.ds(pl.multiple_of(source * 16, 16), 16), :] = rows
    summed = x_ref[...].astype(F32) + y_ref[...].astype(F32) + z_ref[...].astype(F32)
    summed = summed.astype(BF)
    for slot in range(PAIRS):
        group, k = slot // 4, slot % 4
        halves = []
        for m in (2 * group, 2 * group + 1):
            near = jnp.where(core == 0, own_refs[HOPS[m]][k], other_refs[HOPS[m]][k])
            far = jnp.where(core == 0, other_refs[HOPS[k]][m], own_refs[HOPS[k]][m])
            halves.append(jnp.concatenate([near, far], axis=0))
        turned = turned_b if group else turned_a
        low = jnp.where(turned == 0, halves[0], halves[1])
        high = jnp.where(turned == 0, halves[1], halves[0])
        weights = jnp.concatenate([low, high], axis=0)
        columns = pl.ds(pl.multiple_of(scalar_ref[slot] * BLOCK, BLOCK), BLOCK)
        result = jnp.dot(summed, weights, preferred_element_type=F32)
        out_ref[:, columns] = (tokens_ref[:, columns].astype(F32) + result).astype(BF)


def mix(scalars, tokens, along_x, along_y, along_z, weights):
    whole_block = [
        pl.BlockSpec(a.shape, lambda i, p, n=a.ndim: (0,) * n)
        for a in (tokens, along_x, along_y, *along_z)
    ]
    half = weights[0].shape[1]
    out_block = [pl.BlockSpec((4, half, BLOCK), lambda i, p: (0, 0, 3))] * 8
    return pl.pallas_call(
        mix_kernel,
        out_shape=jax.ShapeDtypeStruct(tokens.shape, BF),
        grid_spec=pltpu.PrefetchScalarGridSpec(
            num_scalar_prefetch=1,
            grid=(1,),
            in_specs=whole_block + out_block,
            out_specs=pl.BlockSpec(tokens.shape, lambda i, p: (0, 0)),
            scratch_shapes=[pltpu.VMEM(tokens.shape, BF)],
        ),
        compiler_params=pltpu.CompilerParams(vmem_limit_bytes=61 * 2**20),
        name="mix",
    )(scalars, tokens, along_x, along_y, *along_z, *weights)


def whole(kernel, out, name, scalars=0, scratch=()):
    vmem = pl.BlockSpec(memory_space=pltpu.VMEM)
    smem = pl.BlockSpec(memory_space=pltpu.SMEM)

    def call(*args):
        return pl.pallas_call(
            kernel,
            out_shape=out,
            in_specs=[smem] * scalars + [vmem] * (len(args) - scalars),
            out_specs=vmem,
            scratch_shapes=list(scratch),
            compiler_params=pltpu.CompilerParams(vmem_limit_bytes=24 * 2**20),
            name=name,
        )(*args)

    return call


def reversed_table(table):
    turned = table[:, ::-1]
    return jnp.pad(turned, ((0, 0), (0, BLOCK - turned.shape[1])))


def bias_blocks(table):
    length = (table.shape[1] + 1) // 2
    shape = jax.ShapeDtypeStruct((PAIRS, BLOCK, 2 * BLOCK), F32)
    return whole(functools.partial(bias_kernel, length), shape, f"bias_{length}")(
        reversed_table(table)
    )


def exchange(array, axes):
    return lax.all_to_all(array, axes, split_axis=0, concat_axis=0, tiled=True)


def swap(array, axis):
    return lax.ppermute(array, axis, [(0, 1), (1, 0)])


def together(array, other):
    return lax.optimization_barrier((array, other))[0]


def shards(tokens, w_qkv, w_out, bias_x, bias_y, bias_z):
    features = tokens.shape[-1]
    shape = tokens.shape
    yh, yl = lax.axis_index("yh"), lax.axis_index("yl")
    x, c = lax.axis_index("x"), lax.axis_index("c")
    pair = yl * DIMS[3] + x
    peers = DIMS[0] * DIMS[1]
    zs = DIMS[2] * DIMS[3] * DIMS[4]

    depth = w_qkv.shape[0] // 2
    mine = [
        lax.dynamic_slice(w_qkv, (c * depth, part * features + pair * BLOCK), (depth, BLOCK))
        for part in range(3)
    ]
    mine.append(lax.dynamic_slice(w_out, (c * depth, pair * BLOCK), (depth, BLOCK)))
    mine = jnp.concatenate(mine, axis=1)
    piece = exchange(jnp.broadcast_to(mine[None], (DIMS[1], *mine.shape)), "z")
    piece = piece.reshape(DIMS[1] * depth, 4 * BLOCK)
    flat = tokens.reshape(-1, features)
    rows = flat.shape[0]
    normed = whole(norm_kernel, jax.ShapeDtypeStruct(flat.shape, BF), "norm")(flat)
    blocks_x = bias_blocks(bias_x)
    blocks_y = bias_blocks(bias_y)
    blocks_z = bias_blocks(bias_z)
    normed = together(normed, (blocks_x, blocks_y, blocks_z))
    piece = together(piece, normed)

    y_lines = exchange(normed.reshape(peers, -1, features), GY).reshape(rows, features)
    z_lines = exchange(together(normed, y_lines).reshape(zs, -1, features), GZ)
    z_lines = z_lines.reshape(rows, features)

    tall = piece.shape[0] // 2
    kept = jnp.where(c == 0, piece[:tall], piece[tall:])
    taken = swap(jnp.where(c == 0, piece[tall:], piece[:tall]), "c")
    rows_of = [jnp.where(c == 0, kept, taken), jnp.where(c == 0, taken, kept)]
    rows_of = [r.reshape(-1, depth, 4 * BLOCK) for r in rows_of]
    piece = jnp.stack(rows_of, axis=1).reshape(-1, 4 * BLOCK)
    first = [piece] + [lax.ppermute(piece, ALL, hop_plane(k, 0)) for k in range(1, 4)]
    first = jnp.stack([first[k] for k in HOPS])
    second = [first] + [lax.ppermute(first, ALL, hop_plane(k, 1)) for k in range(1, 4)]
    waits = {1: y_lines, 2: z_lines}
    others = [
        swap(together(second[k], waits[k]) if k in waits else second[k], "c") for k in range(4)
    ]

    columns = (x - jnp.array(HOPS)) % DIMS[3]
    y = yh * 2 + yl
    turned_b = ((y - 1) % 4) // 2
    scalars = jnp.concatenate(
        [yl * 4 + columns, (1 - yl) * 4 + columns, jnp.stack([c, yh, turned_b, yl, x])]
    ).astype(jnp.int32)

    every = (*second, *others)
    (along_y,) = attend((2,), (y_lines,), every, (blocks_y,), scalars)
    z, along_x = attend((3, 1), (z_lines, normed), every, (blocks_z, blocks_x), scalars, (along_y,))
    along_y = exchange(together(along_y, z_lines).reshape(peers, -1, features), GY)
    along_y = along_y.reshape(rows, features)

    z = z.reshape(4, rows // 4, features)
    back = [z[0]] + [lax.ppermute(z[k], ALL, hop_x(k)) for k in range(1, 4)]
    back_c = jnp.stack([b[r : r + 16] for r in (16, 48) for b in back])
    back_c = swap(together(back_c, along_y), "c")
    back_y = jnp.concatenate([jnp.stack([b[32:48] for b in back]), back_c[4:]], axis=0)
    back_y = swap(back_y, "yl")
    mixed = mix(scalars, flat, along_x, along_y, (*back, back_y, back_c), every)
    return mixed.reshape(shape)


def solution(mesh):
    torus = Mesh(mesh.devices.reshape(DIMS), ALL)
    in_specs = (P(None, None, GY, GZ, None), P(GY, None), P(GY, None), P(), P(), P())
    return jax.shard_map(
        shards, mesh=torus, in_specs=in_specs, out_specs=in_specs[0], check_vma=False
    )
```

```python
import functools
import jax
import jax.numpy as jnp
from jax import lax
from jax.experimental import pallas as pl
from jax.experimental.pallas import tpu as pltpu
from jax.sharding import Mesh
from jax.sharding import PartitionSpec as P

HEADS = 16
HEAD = 64
PAIRS = HEADS // 2
BLOCK = 128
NEG = -1e30
HOPS = (0, 2, 1, 3)
DIMS = (2, 16, 2, 4, 2)
ALL = ("yh", "z", "yl", "x", "c")
GY = ("yh", "z")
GZ = ("yl", "x", "c")
BF = jnp.bfloat16
F32 = jnp.float32


def index_of(yh, z, yl, x, c):
    return (((yh * DIMS[1] + z) * DIMS[2] + yl) * DIMS[3] + x) * DIMS[4] + c


def every_device():
    for yh in range(DIMS[0]):
        for z in range(DIMS[1]):
            for yl in range(DIMS[2]):
                for x in range(DIMS[3]):
                    for c in range(DIMS[4]):
                        yield yh, z, yl, x, c


def hop_x(far):
    return [
        (index_of(*d), index_of(d[0], d[1], d[2], (d[3] + far) % DIMS[3], d[4]))
        for d in every_device()
    ]


def hop_plane(far, x_core):
    pairs = []
    for yh, z, yl, x, c in every_device():
        y = yh * 2 + yl
        if c == x_core:
            x_to, y_to = (x + far) % 4, y
        else:
            x_to, y_to = x, (y + far) % 4
        pairs.append((index_of(yh, z, yl, x, c), index_of(y_to // 2, z, y_to % 2, x_to, c)))
    return pairs


def iota(shape, dim):
    return lax.broadcasted_iota(jnp.int32, shape, dim)


def line_rows(axis, i):
    if axis == 1:
        return (i & 128) + (i & 63) * 2 + ((i >> 6) & 1)
    if axis == 2:
        return (i & 31) * 8 + (i >> 5)
    return ((i & 30) << 3) + ((i >> 5) << 1) + (i & 1)


def norm_kernel(tokens_ref, out_ref):
    values = tokens_ref[...].astype(F32)
    center = jnp.mean(values, axis=-1, keepdims=True)
    values = values - center
    spread = jnp.mean(values * values, axis=-1, keepdims=True)
    out_ref[...] = (values * lax.rsqrt(spread + 1e-05)).astype(BF)


def bias_kernel(length, table_ref, out_ref):
    lanes = iota((length, BLOCK), 1) // length
    for head in range(HEADS):
        row = jnp.broadcast_to(table_ref[head : head + 1, :], (length, BLOCK))
        for place in range(BLOCK // length):
            shift = (place * length - length + 1) % BLOCK
            turned = pltpu.roll(row, shift, 1, stride=1, stride_axis=0)
            out_ref[
                head // 2,
                place * length : (place + 1) * length,
                (head % 2) * BLOCK : (head % 2 + 1) * BLOCK,
            ] = jnp.where(lanes == place, turned, NEG)


def attend_kernel(axes, scalar_ref, *refs):
    count = len(axes)
    token_refs, refs = refs[:count], refs[count:]
    weight_refs, refs = refs[:8], refs[8:]
    bias_refs = refs[: 2 * count]
    refs = refs[-(count * 2 + 3) :]
    out_refs, back_refs = refs[:count], refs[count : 2 * count]
    lines_ref, qkv_ref, mixed_ref = refs[2 * count :]
    step = pl.program_id(0)
    rows = token_refs[0].shape[0]
    core, turned_a, turned_b, yl, x = [scalar_ref[8 + n] for n in range(5)]

    @pl.when(step == 0)
    def _():
        for a, axis in enumerate(axes):
            turn = line_rows(axis, iota((rows, 1), 0)) == iota((rows, rows), 1)
            turn = turn.astype(F32).astype(BF)
            lines = jnp.dot(turn, token_refs[a][...], preferred_element_type=F32)
            lines_ref[a * rows : (a + 1) * rows] = lines.astype(BF)
            place = iota((rows, 1), 0)
            if axis == 3:
                dx, dy, dc = place >> 6, (place >> 5) & 1, (place >> 4) & 1
                to = (yl ^ dy) * 8 + ((x + dx) & 3) * 2 + (core ^ dc)
                back = ((place >> 1) & 7) * 32 + to * 2 + (place & 1) == iota((rows, rows), 1)
            else:
                back = line_rows(axis, iota((1, rows), 1)) == iota((rows, rows), 0)
            back_refs[a][...] = back.astype(F32).astype(BF)

    width = 3 * BLOCK

    def attention():
        left = iota((BLOCK, BLOCK), 1) < HEAD
        zero = jnp.zeros((BLOCK, BLOCK), BF)
        projected = (step + 1) % 2
        for n in range(2):
            pair = scalar_ref[2 * jnp.maximum(step - 1, 0) + n]
            columns = pl.ds(pl.multiple_of(pair * BLOCK, BLOCK), BLOCK)
            for start in range(0, count * rows, BLOCK):
                q, k, v = [
                    qkv_ref[
                        projected,
                        start : start + BLOCK,
                        n * width + m * BLOCK : n * width + (m + 1) * BLOCK,
                    ]
                    for m in range(3)
                ]
                keys = jnp.concatenate([jnp.where(left, k, zero), jnp.where(left, zero, k)], axis=0)
                values = jnp.concatenate([jnp.where(left, v, zero), jnp.where(left, zero, v)], axis=0)
                scores = lax.dot_general(q, keys, (((1,), (1,)), ((), ())), preferred_element_type=F32)
                scores = scores * HEAD ** (-0.5) + bias_refs[2 * (start // rows) + n][0]
                probs = []
                for half in range(2):
                    s = scores[:, half * BLOCK : (half + 1) * BLOCK]
                    e = jnp.exp(s - jnp.max(s, axis=-1, keepdims=True))
                    probs.append((e * (1.0 / jnp.sum(e, axis=-1, keepdims=True))).astype(BF))
                probs = jnp.concatenate(probs, axis=1)
                mixed = jnp.dot(probs, values, preferred_element_type=F32).astype(BF)
                mixed_ref[start : start + BLOCK, columns] = mixed

    def projection():
        turned = jnp.where(step < 2, turned_a, turned_b)
        near_first, far_first = step < 2, step % 2 == 0
        own_first = jnp.where(core == 0, near_first, far_first)
        other_first = jnp.where(core == 0, far_first, near_first)
        own_refs, other_refs = weight_refs[:4], weight_refs[4:]
        weights = []
        for n in range(2):
            halves = []
            for m in range(2):
                own, other = [
                    [jnp.where(early, part[2 * i][j], part[2 * i + 1][j]) for i, j in ((m, n), (n, m))]
                    for part, early in ((own_refs, own_first), (other_refs, other_first))
                ]
                near = jnp.where(core == 0, own[0], other[0])
                far = jnp.where(core == 0, other[1], own[1])
                halves.append(jnp.concatenate([near, far], axis=0))
            low = jnp.where(turned == 0, halves[0], halves[1])
            high = jnp.where(turned == 0, halves[1], halves[0])
            weights.append(jnp.concatenate([low, high], axis=0))
        weights = jnp.concatenate(weights, axis=1)
        qkv = jnp.dot(lines_ref[...], weights, preferred_element_type=F32)
        qkv_ref[step % 2] = qkv.astype(BF)

    last = pl.num_programs(0) - 1

    @pl.when(step == 0)
    def _():
        projection()

    @pl.when(jnp.logical_and(step > 0, step < last))
    def _():
        attention()
        projection()

    @pl.when(step == last)
    def _():
        attention()
        for a in range(count):
            mixed = mixed_ref[a * rows : (a + 1) * rows]
            out = jnp.dot(back_refs[a][...], mixed, preferred_element_type=F32)
            out_refs[a][...] = out.astype(BF)


def attend(axes, tokens, weights, biases, scalars, after=()):
    rows, features = tokens[0].shape
    half, width = weights[0].shape[1], 3 * BLOCK
    count = len(axes)
    specs = [pl.BlockSpec((rows, features), lambda s, p: (0, 0))] * count

    for other in range(2):
        for hop in range(4):
            late = hop % 2

            def block(s, p, other=other, late=late):
                s = jnp.minimum(s, 3)
                y_part, x_part = s // 2, s % 2
                near = jnp.where(y_part == late, x_part, 1 - late)
                return (jnp.where(p[8] == other, near, y_part), 0, 0)

            specs.append(pl.BlockSpec((2, half, width), block))
    for _ in range(count):
        for n in range(2):

            def pair(s, p, n=n):
                return (p[2 * jnp.maximum(s - 1, 0) + n], 0, 0)

            specs.append(pl.BlockSpec((1, BLOCK, 2 * BLOCK), pair))
    specs.extend([pl.BlockSpec(memory_space=pl.ANY)] * len(after))
    bias_args = [b for bias in biases for b in (bias, bias)]
    return pl.pallas_call(
        functools.partial(attend_kernel, axes),
        out_shape=[jax.ShapeDtypeStruct((rows, HEADS * HEAD), BF)] * count,
        grid_spec=pltpu.PrefetchScalarGridSpec(
            num_scalar_prefetch=1,
            grid=(5,),
            in_specs=specs,
            out_specs=[pl.BlockSpec((rows, features), lambda s, p: (0, 0))] * count,
            scratch_shapes=[pltpu.VMEM((rows, rows), BF)] * count
            + [
                pltpu.VMEM((count * rows, features), BF),
                pltpu.VMEM((2, count * rows, 2 * width), BF),
                pltpu.VMEM((count * rows, features), BF),
            ],
        ),
        compiler_params=pltpu.CompilerParams(vmem_limit_bytes=61 * 2**20),
        cost_estimate=pl.CostEstimate(flops=1000, bytes_accessed=1000, transcendentals=0),
        name="attend_" + "_".join(map(str, axes)),
    )(scalars, *tokens, *weights, *bias_args, *after)


def gather_kernel(scalar_ref, *refs):
    own_refs, other_refs, out_ref = refs[:4], refs[4:8], refs[-1]
    core, turned_a, turned_b = [scalar_ref[8 + n] for n in range(3)]
    for slot in range(PAIRS):
        group, k = slot // 4, slot % 4
        halves = []
        for m in (2 * group, 2 * group + 1):
            near = jnp.where(core == 0, own_refs[HOPS[m]][k], other_refs[HOPS[m]][k])
            far = jnp.where(core == 0, other_refs[HOPS[k]][m], own_refs[HOPS[k]][m])
            halves.append(jnp.concatenate([near, far], axis=0))
        turned = turned_b if group else turned_a
        low = jnp.where(turned == 0, halves[0], halves[1])
        high = jnp.where(turned == 0, halves[1], halves[0])
        columns = pl.ds(pl.multiple_of(scalar_ref[slot] * BLOCK, BLOCK), BLOCK)
        out_ref[:, columns] = jnp.concatenate([low, high], axis=0)


def gather_out(scalars, weights, after):
    half = weights[0].shape[1]
    size = HEADS * HEAD
    specs = [pl.BlockSpec((4, half, BLOCK), lambda i, p: (0, 0, 3))] * 8
    specs.append(pl.BlockSpec(memory_space=pl.ANY))
    return pl.pallas_call(
        gather_kernel,
        out_shape=jax.ShapeDtypeStruct((size, size), BF),
        grid_spec=pltpu.PrefetchScalarGridSpec(
            num_scalar_prefetch=1,
            grid=(1,),
            in_specs=specs,
            out_specs=pl.BlockSpec((size, size), lambda i, p: (0, 0)),
        ),
        compiler_params=pltpu.CompilerParams(vmem_limit_bytes=24 * 2**20),
        name="gather_out",
    )(scalars, *weights, after)


def mix_kernel(distance, scalar_ref, tokens_ref, x_ref, y_ref, parts_ref, w_ref, *refs):
    out_ref, z_ref = refs[-2:]
    core, yl, x = scalar_ref[8], scalar_ref[11], scalar_ref[12]
    half = z_ref.shape[0]
    for k in range(4):
        for dc in range(2):
            source = ((x - k + 4) & 3) * 2 + (core ^ dc)
            z_ref[pl.ds(pl.multiple_of(source * 16, 16), 16), :] = parts_ref[dc * 4 + k]
    mine = pl.ds(pl.multiple_of((yl ^ distance) * half, half), half)
    summed = x_ref[mine, :].astype(F32) + y_ref[mine, :].astype(F32) + z_ref[...].astype(F32)
    result = jnp.dot(summed.astype(BF), w_ref[...], preferred_element_type=F32)
    result = (tokens_ref[mine, :].astype(F32) + result).astype(BF)
    if distance == 0:
        out_ref[...] = result
    else:
        out_ref[mine, :] = result
        out_ref[pl.ds(pl.multiple_of(yl * half, half), half), :] = refs[0][...]


def mix(distance, shape, scalars, *args):
    half = (args[0].shape[0] // 2, args[0].shape[1])
    return whole(
        functools.partial(mix_kernel, distance),
        jax.ShapeDtypeStruct(shape, BF),
        f"mix_{distance}",
        1,
        [pltpu.VMEM(half, BF)],
    )(scalars, *args)


def whole(kernel, out, name, scalars=0, scratch=()):
    vmem = pl.BlockSpec(memory_space=pltpu.VMEM)
    smem = pl.BlockSpec(memory_space=pltpu.SMEM)

    def call(*args):
        return pl.pallas_call(
            kernel,
            out_shape=out,
            in_specs=[smem] * scalars + [vmem] * (len(args) - scalars),
            out_specs=vmem,
            scratch_shapes=list(scratch),
            compiler_params=pltpu.CompilerParams(vmem_limit_bytes=24 * 2**20),
            name=name,
        )(*args)

    return call


def reversed_table(table):
    turned = table[:, ::-1]
    return jnp.pad(turned, ((0, 0), (0, BLOCK - turned.shape[1])))


def bias_blocks(table):
    length = (table.shape[1] + 1) // 2
    shape = jax.ShapeDtypeStruct((PAIRS, BLOCK, 2 * BLOCK), F32)
    return whole(functools.partial(bias_kernel, length), shape, f"bias_{length}")(
        reversed_table(table)
    )


def exchange(array, axes):
    return lax.all_to_all(array, axes, split_axis=0, concat_axis=0, tiled=True)


def swap(array, axis):
    return lax.ppermute(array, axis, [(0, 1), (1, 0)])


def together(array, other):
    return lax.optimization_barrier((array, other))[0]


def shards(tokens, w_qkv, w_out, bias_x, bias_y, bias_z):
    features = tokens.shape[-1]
    shape = tokens.shape
    yh, yl = lax.axis_index("yh"), lax.axis_index("yl")
    x, c = lax.axis_index("x"), lax.axis_index("c")
    pair = yl * DIMS[3] + x
    peers = DIMS[0] * DIMS[1]
    zs = DIMS[2] * DIMS[3] * DIMS[4]

    depth = w_qkv.shape[0] // 2
    mine = [
        lax.dynamic_slice(w_qkv, (c * depth, part * features + pair * BLOCK), (depth, BLOCK))
        for part in range(3)
    ]
    mine.append(lax.dynamic_slice(w_out, (c * depth, pair * BLOCK), (depth, BLOCK)))
    mine = jnp.concatenate(mine, axis=1)
    piece = exchange(jnp.broadcast_to(mine[None], (DIMS[1], *mine.shape)), "z")
    piece = piece.reshape(DIMS[1] * depth, 4 * BLOCK)
    flat = tokens.reshape(-1, features)
    rows = flat.shape[0]
    normed = whole(norm_kernel, jax.ShapeDtypeStruct(flat.shape, BF), "norm")(flat)
    blocks_x = bias_blocks(bias_x)
    blocks_y = bias_blocks(bias_y)
    blocks_z = bias_blocks(bias_z)
    normed = together(normed, (blocks_x, blocks_y, blocks_z))
    piece = together(piece, normed)

    y_lines = exchange(normed.reshape(peers, -1, features), GY).reshape(rows, features)
    z_lines = exchange(together(normed, y_lines).reshape(zs, -1, features), GZ)
    z_lines = z_lines.reshape(rows, features)

    tall = piece.shape[0] // 2
    kept = jnp.where(c == 0, piece[:tall], piece[tall:])
    taken = swap(jnp.where(c == 0, piece[tall:], piece[:tall]), "c")
    rows_of = [jnp.where(c == 0, kept, taken), jnp.where(c == 0, taken, kept)]
    rows_of = [r.reshape(-1, depth, 4 * BLOCK) for r in rows_of]
    piece = jnp.stack(rows_of, axis=1).reshape(-1, 4 * BLOCK)
    first = [piece] + [lax.ppermute(piece, ALL, hop_plane(k, 0)) for k in range(1, 4)]
    first = jnp.stack([first[k] for k in HOPS])
    second = [first] + [lax.ppermute(first, ALL, hop_plane(k, 1)) for k in range(1, 4)]
    waits = {1: y_lines, 2: z_lines}
    others = [
        swap(together(second[k], waits[k]) if k in waits else second[k], "c") for k in range(4)
    ]

    columns = (x - jnp.array(HOPS)) % DIMS[3]
    y = yh * 2 + yl
    turned_b = ((y - 1) % 4) // 2
    scalars = jnp.concatenate(
        [yl * 4 + columns, (1 - yl) * 4 + columns, jnp.stack([c, yh, turned_b, yl, x])]
    ).astype(jnp.int32)

    every = (*second, *others)
    along_y, z = attend((2, 3), (y_lines, z_lines), every, (blocks_y, blocks_z), scalars)
    along_y = exchange(along_y.reshape(peers, -1, features), GY).reshape(rows, features)

    z = z.reshape(4, rows // 4, features)
    back = [z[0]] + [lax.ppermute(z[k], ALL, hop_x(k)) for k in range(1, 4)]
    (along_x,) = attend((1,), (normed,), every, (blocks_x,), scalars)
    w_whole = gather_out(scalars, every, along_x)
    back_c = jnp.stack([b[r : r + 16] for r in (16, 48) for b in back])
    back_c = swap(together(back_c, (along_y, w_whole)), "c")
    back_y = jnp.concatenate([jnp.stack([b[32:48] for b in back]), back_c[4:]], axis=0)
    back_y = swap(back_y, "yl")
    near_z = jnp.concatenate([jnp.stack([b[:16] for b in back]), back_c[:4]], axis=0)
    mixed = mix(0, (rows // 2, features), scalars, flat, along_x, along_y, near_z, w_whole)
    mixed = mix(1, flat.shape, scalars, flat, along_x, along_y, back_y, w_whole, mixed)
    return mixed.reshape(shape)


def solution(mesh):
    torus = Mesh(mesh.devices.reshape(DIMS), ALL)
    in_specs = (P(None, None, GY, GZ, None), P(GY, None), P(GY, None), P(), P(), P())
    return jax.shard_map(
        shards, mesh=torus, in_specs=in_specs, out_specs=in_specs[0], check_vma=False
    )
```

```python
import functools
import jax
import jax.numpy as jnp
from jax import lax
from jax.experimental import pallas as pl
from jax.experimental.pallas import tpu as pltpu
from jax.sharding import Mesh
from jax.sharding import PartitionSpec as P

HEADS = 16
HEAD = 64
PAIRS = HEADS // 2
BLOCK = 128
NEG = -1e30
HOPS = (0, 2, 1, 3)
DIMS = (2, 16, 2, 4, 2)
ALL = ("yh", "z", "yl", "x", "c")
GY = ("yh", "z")
GZ = ("yl", "x", "c")
BF = jnp.bfloat16
F32 = jnp.float32


def index_of(yh, z, yl, x, c):
    return (((yh * DIMS[1] + z) * DIMS[2] + yl) * DIMS[3] + x) * DIMS[4] + c


def every_device():
    for yh in range(DIMS[0]):
        for z in range(DIMS[1]):
            for yl in range(DIMS[2]):
                for x in range(DIMS[3]):
                    for c in range(DIMS[4]):
                        yield yh, z, yl, x, c


def hop_x(far):
    return [
        (index_of(*d), index_of(d[0], d[1], d[2], (d[3] + far) % DIMS[3], d[4]))
        for d in every_device()
    ]


def hop_plane(far, x_core):
    pairs = []
    for yh, z, yl, x, c in every_device():
        y = yh * 2 + yl
        if c == x_core:
            x_to, y_to = (x + far) % 4, y
        else:
            x_to, y_to = x, (y + far) % 4
        pairs.append((index_of(yh, z, yl, x, c), index_of(y_to // 2, z, y_to % 2, x_to, c)))
    return pairs


def iota(shape, dim):
    return lax.broadcasted_iota(jnp.int32, shape, dim)


def line_rows(axis, i):
    if axis == 1:
        return (i & 128) + (i & 63) * 2 + ((i >> 6) & 1)
    if axis == 2:
        return (i & 31) * 8 + (i >> 5)
    return ((i & 30) << 3) + ((i >> 5) << 1) + (i & 1)


def norm_kernel(tokens_ref, out_ref):
    values = tokens_ref[...].astype(F32)
    center = jnp.mean(values, axis=-1, keepdims=True)
    values = values - center
    spread = jnp.mean(values * values, axis=-1, keepdims=True)
    out_ref[...] = (values * lax.rsqrt(spread + 1e-05)).astype(BF)


def bias_kernel(length, table_ref, out_ref):
    lanes = iota((length, BLOCK), 1) // length
    for head in range(HEADS):
        row = jnp.broadcast_to(table_ref[head : head + 1, :], (length, BLOCK))
        for place in range(BLOCK // length):
            shift = (place * length - length + 1) % BLOCK
            turned = pltpu.roll(row, shift, 1, stride=1, stride_axis=0)
            out_ref[
                head // 2,
                place * length : (place + 1) * length,
                (head % 2) * BLOCK : (head % 2 + 1) * BLOCK,
            ] = jnp.where(lanes == place, turned, NEG)


def attend_kernel(axes, scalar_ref, *refs):
    count = len(axes)
    token_refs, refs = refs[:count], refs[count:]
    weight_refs, refs = refs[:8], refs[8:]
    bias_refs = refs[: 2 * count]
    refs = refs[-(count * 2 + 3) :]
    out_refs, back_refs = refs[:count], refs[count : 2 * count]
    lines_ref, qkv_ref, mixed_ref = refs[2 * count :]
    step = pl.program_id(0)
    rows = token_refs[0].shape[0]
    core, turned_a, turned_b, yl, x = [scalar_ref[8 + n] for n in range(5)]

    @pl.when(step == 0)
    def _():
        for a, axis in enumerate(axes):
            turn = line_rows(axis, iota((rows, 1), 0)) == iota((rows, rows), 1)
            turn = turn.astype(F32).astype(BF)
            lines = jnp.dot(turn, token_refs[a][...], preferred_element_type=F32)
            lines_ref[a * rows : (a + 1) * rows] = lines.astype(BF)
            place = iota((rows, 1), 0)
            if axis == 3:
                dx, dy, dc = place >> 6, (place >> 5) & 1, (place >> 4) & 1
                to = (yl ^ dy) * 8 + ((x + dx) & 3) * 2 + (core ^ dc)
                back = ((place >> 1) & 7) * 32 + to * 2 + (place & 1) == iota((rows, rows), 1)
            else:
                back = line_rows(axis, iota((1, rows), 1)) == iota((rows, rows), 0)
            back_refs[a][...] = back.astype(F32).astype(BF)

    width = 3 * BLOCK

    def attention():
        left = iota((BLOCK, BLOCK), 1) < HEAD
        zero = jnp.zeros((BLOCK, BLOCK), BF)
        projected = (step + 1) % 2
        for n in range(2):
            pair = scalar_ref[2 * jnp.maximum(step - 1, 0) + n]
            columns = pl.ds(pl.multiple_of(pair * BLOCK, BLOCK), BLOCK)
            for start in range(0, count * rows, BLOCK):
                q, k, v = [
                    qkv_ref[
                        projected,
                        start : start + BLOCK,
                        n * width + m * BLOCK : n * width + (m + 1) * BLOCK,
                    ]
                    for m in range(3)
                ]
                keys = jnp.concatenate([jnp.where(left, k, zero), jnp.where(left, zero, k)], axis=0)
                values = jnp.concatenate([jnp.where(left, v, zero), jnp.where(left, zero, v)], axis=0)
                scores = lax.dot_general(q, keys, (((1,), (1,)), ((), ())), preferred_element_type=F32)
                scores = scores * HEAD ** (-0.5) + bias_refs[2 * (start // rows) + n][0]
                probs = []
                for half in range(2):
                    s = scores[:, half * BLOCK : (half + 1) * BLOCK]
                    e = jnp.exp(s - jnp.max(s, axis=-1, keepdims=True))
                    probs.append((e * (1.0 / jnp.sum(e, axis=-1, keepdims=True))).astype(BF))
                probs = jnp.concatenate(probs, axis=1)
                mixed = jnp.dot(probs, values, preferred_element_type=F32).astype(BF)
                mixed_ref[start : start + BLOCK, columns] = mixed

    def projection():
        turned = jnp.where(step < 2, turned_a, turned_b)
        near_first, far_first = step < 2, step % 2 == 0
        own_first = jnp.where(core == 0, near_first, far_first)
        other_first = jnp.where(core == 0, far_first, near_first)
        own_refs, other_refs = weight_refs[:4], weight_refs[4:]
        weights = []
        for n in range(2):
            halves = []
            for m in range(2):
                own, other = [
                    [jnp.where(early, part[2 * i][j], part[2 * i + 1][j]) for i, j in ((m, n), (n, m))]
                    for part, early in ((own_refs, own_first), (other_refs, other_first))
                ]
                near = jnp.where(core == 0, own[0], other[0])
                far = jnp.where(core == 0, other[1], own[1])
                halves.append(jnp.concatenate([near, far], axis=0))
            low = jnp.where(turned == 0, halves[0], halves[1])
            high = jnp.where(turned == 0, halves[1], halves[0])
            weights.append(jnp.concatenate([low, high], axis=0))
        weights = jnp.concatenate(weights, axis=1)
        qkv = jnp.dot(lines_ref[...], weights, preferred_element_type=F32)
        qkv_ref[step % 2] = qkv.astype(BF)

    last = pl.num_programs(0) - 1

    @pl.when(step == 0)
    def _():
        projection()

    @pl.when(jnp.logical_and(step > 0, step < last))
    def _():
        attention()
        projection()

    @pl.when(step == last)
    def _():
        attention()
        for a in range(count):
            mixed = mixed_ref[a * rows : (a + 1) * rows]
            out = jnp.dot(back_refs[a][...], mixed, preferred_element_type=F32)
            out_refs[a][...] = out.astype(BF)


def attend(axes, tokens, weights, biases, scalars, after=()):
    rows, features = tokens[0].shape
    half, width = weights[0].shape[1], 3 * BLOCK
    count = len(axes)
    specs = [pl.BlockSpec((rows, features), lambda s, p: (0, 0))] * count

    for other in range(2):
        for hop in range(4):
            late = hop % 2

            def block(s, p, other=other, late=late):
                s = jnp.minimum(s, 3)
                y_part, x_part = s // 2, s % 2
                near = jnp.where(y_part == late, x_part, 1 - late)
                return (jnp.where(p[8] == other, near, y_part), 0, 0)

            specs.append(pl.BlockSpec((2, half, width), block))
    for _ in range(count):
        for n in range(2):

            def pair(s, p, n=n):
                return (p[2 * jnp.maximum(s - 1, 0) + n], 0, 0)

            specs.append(pl.BlockSpec((1, BLOCK, 2 * BLOCK), pair))
    specs.extend([pl.BlockSpec(memory_space=pl.ANY)] * len(after))
    bias_args = [b for bias in biases for b in (bias, bias)]
    return pl.pallas_call(
        functools.partial(attend_kernel, axes),
        out_shape=[jax.ShapeDtypeStruct((rows, HEADS * HEAD), BF)] * count,
        grid_spec=pltpu.PrefetchScalarGridSpec(
            num_scalar_prefetch=1,
            grid=(5,),
            in_specs=specs,
            out_specs=[pl.BlockSpec((rows, features), lambda s, p: (0, 0))] * count,
            scratch_shapes=[pltpu.VMEM((rows, rows), BF)] * count
            + [
                pltpu.VMEM((count * rows, features), BF),
                pltpu.VMEM((2, count * rows, 2 * width), BF),
                pltpu.VMEM((count * rows, features), BF),
            ],
        ),
        compiler_params=pltpu.CompilerParams(vmem_limit_bytes=61 * 2**20),
        cost_estimate=pl.CostEstimate(flops=1000, bytes_accessed=1000, transcendentals=0),
        name="attend_" + "_".join(map(str, axes)),
    )(scalars, *tokens, *weights, *bias_args, *after)


def gather_kernel(scalar_ref, *refs):
    own_refs, other_refs, out_ref = refs[:4], refs[4:8], refs[-1]
    core, turned_a, turned_b = [scalar_ref[8 + n] for n in range(3)]
    for slot in range(PAIRS):
        group, k = slot // 4, slot % 4
        halves = []
        for m in (2 * group, 2 * group + 1):
            near = jnp.where(core == 0, own_refs[HOPS[m]][k], other_refs[HOPS[m]][k])
            far = jnp.where(core == 0, other_refs[HOPS[k]][m], own_refs[HOPS[k]][m])
            halves.append(jnp.concatenate([near, far], axis=0))
        turned = turned_b if group else turned_a
        low = jnp.where(turned == 0, halves[0], halves[1])
        high = jnp.where(turned == 0, halves[1], halves[0])
        columns = pl.ds(pl.multiple_of(scalar_ref[slot] * BLOCK, BLOCK), BLOCK)
        out_ref[:, columns] = jnp.concatenate([low, high], axis=0)


def gather_out(scalars, weights, after):
    half = weights[0].shape[1]
    size = HEADS * HEAD
    specs = [pl.BlockSpec((4, half, BLOCK), lambda i, p: (0, 0, 3))] * 8
    specs.append(pl.BlockSpec(memory_space=pl.ANY))
    return pl.pallas_call(
        gather_kernel,
        out_shape=jax.ShapeDtypeStruct((size, size), BF),
        grid_spec=pltpu.PrefetchScalarGridSpec(
            num_scalar_prefetch=1,
            grid=(1,),
            in_specs=specs,
            out_specs=pl.BlockSpec((size, size), lambda i, p: (0, 0)),
        ),
        compiler_params=pltpu.CompilerParams(vmem_limit_bytes=24 * 2**20),
        cost_estimate=pl.CostEstimate(flops=1000, bytes_accessed=1000, transcendentals=0),
        name="gather_out",
    )(scalars, *weights, after)


def mix_kernel(distance, scalar_ref, tokens_ref, x_ref, y_ref, parts_ref, w_ref, *refs):
    out_ref, z_ref = refs[-2:]
    core, yl, x = scalar_ref[8], scalar_ref[11], scalar_ref[12]
    half = z_ref.shape[0]
    for k in range(4):
        for dc in range(2):
            source = ((x - k + 4) & 3) * 2 + (core ^ dc)
            z_ref[pl.ds(pl.multiple_of(source * 16, 16), 16), :] = parts_ref[dc * 4 + k]
    mine = pl.ds(pl.multiple_of((yl ^ distance) * half, half), half)
    summed = x_ref[mine, :].astype(F32) + y_ref[mine, :].astype(F32) + z_ref[...].astype(F32)
    result = jnp.dot(summed.astype(BF), w_ref[...], preferred_element_type=F32)
    result = (tokens_ref[mine, :].astype(F32) + result).astype(BF)
    if distance == 0:
        out_ref[...] = result
    else:
        out_ref[mine, :] = result
        out_ref[pl.ds(pl.multiple_of(yl * half, half), half), :] = refs[0][...]


def mix(distance, shape, scalars, *args):
    half = (args[0].shape[0] // 2, args[0].shape[1])
    return whole(
        functools.partial(mix_kernel, distance),
        jax.ShapeDtypeStruct(shape, BF),
        f"mix_{distance}",
        1,
        [pltpu.VMEM(half, BF)],
    )(scalars, *args)


def whole(kernel, out, name, scalars=0, scratch=()):
    vmem = pl.BlockSpec(memory_space=pltpu.VMEM)
    smem = pl.BlockSpec(memory_space=pltpu.SMEM)

    def call(*args):
        return pl.pallas_call(
            kernel,
            out_shape=out,
            in_specs=[smem] * scalars + [vmem] * (len(args) - scalars),
            out_specs=vmem,
            scratch_shapes=list(scratch),
            compiler_params=pltpu.CompilerParams(vmem_limit_bytes=24 * 2**20),
            name=name,
        )(*args)

    return call


def reversed_table(table):
    turned = table[:, ::-1]
    return jnp.pad(turned, ((0, 0), (0, BLOCK - turned.shape[1])))


def bias_blocks(table):
    length = (table.shape[1] + 1) // 2
    shape = jax.ShapeDtypeStruct((PAIRS, BLOCK, 2 * BLOCK), F32)
    return whole(functools.partial(bias_kernel, length), shape, f"bias_{length}")(
        reversed_table(table)
    )


def exchange(array, axes):
    return lax.all_to_all(array, axes, split_axis=0, concat_axis=0, tiled=True)


def swap(array, axis):
    return lax.ppermute(array, axis, [(0, 1), (1, 0)])


def together(array, other):
    return lax.optimization_barrier((array, other))[0]


def shards(tokens, w_qkv, w_out, bias_x, bias_y, bias_z):
    features = tokens.shape[-1]
    shape = tokens.shape
    yh, yl = lax.axis_index("yh"), lax.axis_index("yl")
    x, c = lax.axis_index("x"), lax.axis_index("c")
    pair = yl * DIMS[3] + x
    peers = DIMS[0] * DIMS[1]
    zs = DIMS[2] * DIMS[3] * DIMS[4]

    depth = w_qkv.shape[0] // 2
    mine = [
        lax.dynamic_slice(w_qkv, (c * depth, part * features + pair * BLOCK), (depth, BLOCK))
        for part in range(3)
    ]
    mine.append(lax.dynamic_slice(w_out, (c * depth, pair * BLOCK), (depth, BLOCK)))
    mine = jnp.concatenate(mine, axis=1)
    piece = exchange(jnp.broadcast_to(mine[None], (DIMS[1], *mine.shape)), "z")
    piece = piece.reshape(DIMS[1] * depth, 4 * BLOCK)
    flat = tokens.reshape(-1, features)
    rows = flat.shape[0]
    normed = whole(norm_kernel, jax.ShapeDtypeStruct(flat.shape, BF), "norm")(flat)
    blocks_x = bias_blocks(bias_x)
    blocks_y = bias_blocks(bias_y)
    blocks_z = bias_blocks(bias_z)
    normed = together(normed, (blocks_x, blocks_y, blocks_z))
    piece = together(piece, normed)

    y_lines = exchange(normed.reshape(peers, -1, features), GY).reshape(rows, features)
    z_lines = exchange(together(normed, y_lines).reshape(zs, -1, features), GZ)
    z_lines = z_lines.reshape(rows, features)

    tall = piece.shape[0] // 2
    kept = jnp.where(c == 0, piece[:tall], piece[tall:])
    taken = swap(jnp.where(c == 0, piece[tall:], piece[:tall]), "c")
    rows_of = [jnp.where(c == 0, kept, taken), jnp.where(c == 0, taken, kept)]
    rows_of = [r.reshape(-1, depth, 4 * BLOCK) for r in rows_of]
    piece = jnp.stack(rows_of, axis=1).reshape(-1, 4 * BLOCK)
    first = [piece] + [lax.ppermute(piece, ALL, hop_plane(k, 0)) for k in range(1, 4)]
    first = jnp.stack([first[k] for k in HOPS])
    second = [first] + [lax.ppermute(first, ALL, hop_plane(k, 1)) for k in range(1, 4)]
    waits = {1: y_lines, 2: z_lines}
    others = [
        swap(together(second[k], waits[k]) if k in waits else second[k], "c") for k in range(4)
    ]

    columns = (x - jnp.array(HOPS)) % DIMS[3]
    y = yh * 2 + yl
    turned_b = ((y - 1) % 4) // 2
    scalars = jnp.concatenate(
        [yl * 4 + columns, (1 - yl) * 4 + columns, jnp.stack([c, yh, turned_b, yl, x])]
    ).astype(jnp.int32)

    every = (*second, *others)
    along_y, z = attend((2, 3), (y_lines, z_lines), every, (blocks_y, blocks_z), scalars)
    along_y = exchange(along_y.reshape(peers, -1, features), GY).reshape(rows, features)

    z = z.reshape(4, rows // 4, features)
    back = [z[0]] + [lax.ppermute(z[k], ALL, hop_x(k)) for k in range(1, 4)]
    (along_x,) = attend((1,), (normed,), every, (blocks_x,), scalars)
    w_whole = gather_out(scalars, every, along_x)
    far_c = swap(jnp.stack([b[48:] for b in back]), "c")
    back_y = jnp.concatenate([jnp.stack([b[32:48] for b in back]), far_c], axis=0)
    back_y = swap(back_y, "yl")
    near_c = swap(jnp.stack([b[16:32] for b in back]), "c")
    near_z = jnp.concatenate([jnp.stack([b[:16] for b in back]), near_c], axis=0)
    mixed = mix(0, (rows // 2, features), scalars, flat, along_x, along_y, near_z, w_whole)
    mixed = mix(1, flat.shape, scalars, flat, along_x, along_y, back_y, w_whole, mixed)
    return mixed.reshape(shape)


def solution(mesh):
    torus = Mesh(mesh.devices.reshape(DIMS), ALL)
    in_specs = (P(None, None, GY, GZ, None), P(GY, None), P(GY, None), P(), P(), P())
    return jax.shard_map(
        shards, mesh=torus, in_specs=in_specs, out_specs=in_specs[0], check_vma=False
    )
```

```python
import functools
import jax
import jax.numpy as jnp
from jax import lax
from jax.experimental import pallas as pl
from jax.experimental.pallas import tpu as pltpu
from jax.sharding import Mesh
from jax.sharding import PartitionSpec as P

HEADS = 16
HEAD = 64
PAIRS = HEADS // 2
BLOCK = 128
NEG = -1e30
HOPS = (0, 2, 1, 3)
DIMS = (2, 16, 2, 4, 2)
ALL = ("yh", "z", "yl", "x", "c")
GY = ("yh", "z")
GZ = ("yl", "x", "c")
BF = jnp.bfloat16
F32 = jnp.float32


def index_of(yh, z, yl, x, c):
    return (((yh * DIMS[1] + z) * DIMS[2] + yl) * DIMS[3] + x) * DIMS[4] + c


def every_device():
    for yh in range(DIMS[0]):
        for z in range(DIMS[1]):
            for yl in range(DIMS[2]):
                for x in range(DIMS[3]):
                    for c in range(DIMS[4]):
                        yield yh, z, yl, x, c


def hop_x(far):
    return [
        (index_of(*d), index_of(d[0], d[1], d[2], (d[3] + far) % DIMS[3], d[4]))
        for d in every_device()
    ]


def hop_plane(far, x_core):
    pairs = []
    for yh, z, yl, x, c in every_device():
        y = yh * 2 + yl
        if c == x_core:
            x_to, y_to = (x + far) % 4, y
        else:
            x_to, y_to = x, (y + far) % 4
        pairs.append((index_of(yh, z, yl, x, c), index_of(y_to // 2, z, y_to % 2, x_to, c)))
    return pairs


def iota(shape, dim):
    return lax.broadcasted_iota(jnp.int32, shape, dim)


def line_rows(axis, i):
    if axis == 1:
        return (i & 128) + (i & 63) * 2 + ((i >> 6) & 1)
    if axis == 2:
        return (i & 31) * 8 + (i >> 5)
    return ((i & 30) << 3) + ((i >> 5) << 1) + (i & 1)


def norm_kernel(tokens_ref, out_ref):
    values = tokens_ref[...].astype(F32)
    center = jnp.mean(values, axis=-1, keepdims=True)
    values = values - center
    spread = jnp.mean(values * values, axis=-1, keepdims=True)
    out_ref[...] = (values * lax.rsqrt(spread + 1e-05)).astype(BF)


def bias_kernel(length, table_ref, out_ref):
    lanes = iota((length, BLOCK), 1) // length
    for head in range(HEADS):
        row = jnp.broadcast_to(table_ref[head : head + 1, :], (length, BLOCK))
        for place in range(BLOCK // length):
            shift = (place * length - length + 1) % BLOCK
            turned = pltpu.roll(row, shift, 1, stride=1, stride_axis=0)
            out_ref[
                head // 2,
                place * length : (place + 1) * length,
                (head % 2) * BLOCK : (head % 2 + 1) * BLOCK,
            ] = jnp.where(lanes == place, turned, NEG)


def attend_kernel(axes, scalar_ref, *refs):
    count = len(axes)
    token_refs, refs = refs[:count], refs[count:]
    weight_refs, refs = refs[:8], refs[8:]
    bias_refs = refs[: 2 * count]
    refs = refs[-(count * 2 + 3) :]
    out_refs, back_refs = refs[:count], refs[count : 2 * count]
    lines_ref, qkv_ref, mixed_ref = refs[2 * count :]
    step = pl.program_id(0)
    rows = token_refs[0].shape[0]
    core, turned_a, turned_b, yl, x = [scalar_ref[8 + n] for n in range(5)]

    @pl.when(step == 0)
    def _():
        for a, axis in enumerate(axes):
            turn = line_rows(axis, iota((rows, 1), 0)) == iota((rows, rows), 1)
            turn = turn.astype(F32).astype(BF)
            lines = jnp.dot(turn, token_refs[a][...], preferred_element_type=F32)
            lines_ref[a * rows : (a + 1) * rows] = lines.astype(BF)
            place = iota((rows, 1), 0)
            if axis == 3:
                dx, dy, dc = place >> 6, (place >> 5) & 1, (place >> 4) & 1
                to = (yl ^ dy) * 8 + ((x + dx) & 3) * 2 + (core ^ dc)
                back = ((place >> 1) & 7) * 32 + to * 2 + (place & 1) == iota((rows, rows), 1)
            else:
                back = line_rows(axis, iota((1, rows), 1)) == iota((rows, rows), 0)
            back_refs[a][...] = back.astype(F32).astype(BF)

    width = 3 * BLOCK

    def attention():
        left = iota((BLOCK, BLOCK), 1) < HEAD
        zero = jnp.zeros((BLOCK, BLOCK), BF)
        projected = (step + 1) % 2
        for n in range(2):
            pair = scalar_ref[2 * jnp.maximum(step - 1, 0) + n]
            columns = pl.ds(pl.multiple_of(pair * BLOCK, BLOCK), BLOCK)
            for start in range(0, count * rows, BLOCK):
                q, k, v = [
                    qkv_ref[
                        projected,
                        start : start + BLOCK,
                        n * width + m * BLOCK : n * width + (m + 1) * BLOCK,
                    ]
                    for m in range(3)
                ]
                keys = jnp.concatenate([jnp.where(left, k, zero), jnp.where(left, zero, k)], axis=0)
                values = jnp.concatenate([jnp.where(left, v, zero), jnp.where(left, zero, v)], axis=0)
                scores = lax.dot_general(q, keys, (((1,), (1,)), ((), ())), preferred_element_type=F32)
                scores = scores * HEAD ** (-0.5) + bias_refs[2 * (start // rows) + n][0]
                probs = []
                for half in range(2):
                    s = scores[:, half * BLOCK : (half + 1) * BLOCK]
                    e = jnp.exp(s - jnp.max(s, axis=-1, keepdims=True))
                    probs.append((e * (1.0 / jnp.sum(e, axis=-1, keepdims=True))).astype(BF))
                probs = jnp.concatenate(probs, axis=1)
                mixed = jnp.dot(probs, values, preferred_element_type=F32).astype(BF)
                mixed_ref[start : start + BLOCK, columns] = mixed

    def projection():
        turned = jnp.where(step < 2, turned_a, turned_b)
        near_first, far_first = step < 2, step % 2 == 0
        own_first = jnp.where(core == 0, near_first, far_first)
        other_first = jnp.where(core == 0, far_first, near_first)
        own_refs, other_refs = weight_refs[:4], weight_refs[4:]
        weights = []
        for n in range(2):
            halves = []
            for m in range(2):
                own, other = [
                    [jnp.where(early, part[2 * i][j], part[2 * i + 1][j]) for i, j in ((m, n), (n, m))]
                    for part, early in ((own_refs, own_first), (other_refs, other_first))
                ]
                near = jnp.where(core == 0, own[0], other[0])
                far = jnp.where(core == 0, other[1], own[1])
                halves.append(jnp.concatenate([near, far], axis=0))
            low = jnp.where(turned == 0, halves[0], halves[1])
            high = jnp.where(turned == 0, halves[1], halves[0])
            weights.append(jnp.concatenate([low, high], axis=0))
        weights = jnp.concatenate(weights, axis=1)
        qkv = jnp.dot(lines_ref[...], weights, preferred_element_type=F32)
        qkv_ref[step % 2] = qkv.astype(BF)

    last = pl.num_programs(0) - 1

    @pl.when(step == 0)
    def _():
        projection()

    @pl.when(jnp.logical_and(step > 0, step < last))
    def _():
        attention()
        projection()

    @pl.when(step == last)
    def _():
        attention()
        for a in range(count):
            mixed = mixed_ref[a * rows : (a + 1) * rows]
            out = jnp.dot(back_refs[a][...], mixed, preferred_element_type=F32)
            out_refs[a][...] = out.astype(BF)


def attend(axes, tokens, weights, biases, scalars, after=()):
    rows, features = tokens[0].shape
    half, width = weights[0].shape[1], 3 * BLOCK
    count = len(axes)
    specs = [pl.BlockSpec((rows, features), lambda s, p: (0, 0))] * count

    for other in range(2):
        for hop in range(4):
            late = hop % 2

            def block(s, p, other=other, late=late):
                s = jnp.minimum(s, 3)
                y_part, x_part = s // 2, s % 2
                near = jnp.where(y_part == late, x_part, 1 - late)
                return (jnp.where(p[8] == other, near, y_part), 0, 0)

            specs.append(pl.BlockSpec((2, half, width), block))
    for _ in range(count):
        for n in range(2):

            def pair(s, p, n=n):
                return (p[2 * jnp.maximum(s - 1, 0) + n], 0, 0)

            specs.append(pl.BlockSpec((1, BLOCK, 2 * BLOCK), pair))
    specs.extend([pl.BlockSpec(memory_space=pl.ANY)] * len(after))
    bias_args = [b for bias in biases for b in (bias, bias)]
    return pl.pallas_call(
        functools.partial(attend_kernel, axes),
        out_shape=[jax.ShapeDtypeStruct((rows, HEADS * HEAD), BF)] * count,
        grid_spec=pltpu.PrefetchScalarGridSpec(
            num_scalar_prefetch=1,
            grid=(5,),
            in_specs=specs,
            out_specs=[pl.BlockSpec((rows, features), lambda s, p: (0, 0))] * count,
            scratch_shapes=[pltpu.VMEM((rows, rows), BF)] * count
            + [
                pltpu.VMEM((count * rows, features), BF),
                pltpu.VMEM((2, count * rows, 2 * width), BF),
                pltpu.VMEM((count * rows, features), BF),
            ],
        ),
        compiler_params=pltpu.CompilerParams(vmem_limit_bytes=61 * 2**20),
        cost_estimate=pl.CostEstimate(
            flops=10**10 if axes == (1,) else 1000, bytes_accessed=1000, transcendentals=0
        ),
        name="attend_" + "_".join(map(str, axes)),
    )(scalars, *tokens, *weights, *bias_args, *after)


def gather_kernel(scalar_ref, *refs):
    own_refs, other_refs, out_ref = refs[:4], refs[4:8], refs[-1]
    core, turned_a, turned_b = [scalar_ref[8 + n] for n in range(3)]
    for slot in range(PAIRS):
        group, k = slot // 4, slot % 4
        halves = []
        for m in (2 * group, 2 * group + 1):
            near = jnp.where(core == 0, own_refs[HOPS[m]][k], other_refs[HOPS[m]][k])
            far = jnp.where(core == 0, other_refs[HOPS[k]][m], own_refs[HOPS[k]][m])
            halves.append(jnp.concatenate([near, far], axis=0))
        turned = turned_b if group else turned_a
        low = jnp.where(turned == 0, halves[0], halves[1])
        high = jnp.where(turned == 0, halves[1], halves[0])
        columns = pl.ds(pl.multiple_of(scalar_ref[slot] * BLOCK, BLOCK), BLOCK)
        out_ref[:, columns] = jnp.concatenate([low, high], axis=0)


def gather_out(scalars, weights, after):
    half = weights[0].shape[1]
    size = HEADS * HEAD
    specs = [pl.BlockSpec((4, half, BLOCK), lambda i, p: (0, 0, 3))] * 8
    specs.append(pl.BlockSpec(memory_space=pl.ANY))
    return pl.pallas_call(
        gather_kernel,
        out_shape=jax.ShapeDtypeStruct((size, size), BF),
        grid_spec=pltpu.PrefetchScalarGridSpec(
            num_scalar_prefetch=1,
            grid=(1,),
            in_specs=specs,
            out_specs=pl.BlockSpec((size, size), lambda i, p: (0, 0)),
        ),
        compiler_params=pltpu.CompilerParams(vmem_limit_bytes=61 * 2**20),
        cost_estimate=pl.CostEstimate(flops=3 * 10**9, bytes_accessed=1000, transcendentals=0),
        name="gather_out",
    )(scalars, *weights, after)


def mix_kernel(distance, scalar_ref, tokens_ref, x_ref, y_ref, parts_ref, w_ref, *refs):
    out_ref, z_ref = refs[-2:]
    core, yl, x = scalar_ref[8], scalar_ref[11], scalar_ref[12]
    half = z_ref.shape[0]
    for k in range(4):
        for dc in range(2):
            source = ((x - k + 4) & 3) * 2 + (core ^ dc)
            z_ref[pl.ds(pl.multiple_of(source * 16, 16), 16), :] = parts_ref[dc * 4 + k]
    mine = pl.ds(pl.multiple_of((yl ^ distance) * half, half), half)
    summed = x_ref[mine, :].astype(F32) + y_ref[mine, :].astype(F32) + z_ref[...].astype(F32)
    result = jnp.dot(summed.astype(BF), w_ref[...], preferred_element_type=F32)
    result = (tokens_ref[mine, :].astype(F32) + result).astype(BF)
    if distance == 0:
        out_ref[...] = result
    else:
        out_ref[mine, :] = result
        out_ref[pl.ds(pl.multiple_of(yl * half, half), half), :] = refs[0][...]


def mix(distance, shape, scalars, *args):
    half = (args[0].shape[0] // 2, args[0].shape[1])
    return whole(
        functools.partial(mix_kernel, distance),
        jax.ShapeDtypeStruct(shape, BF),
        f"mix_{distance}",
        1,
        [pltpu.VMEM(half, BF)],
    )(scalars, *args)


def whole(kernel, out, name, scalars=0, scratch=()):
    vmem = pl.BlockSpec(memory_space=pltpu.VMEM)
    smem = pl.BlockSpec(memory_space=pltpu.SMEM)

    def call(*args):
        return pl.pallas_call(
            kernel,
            out_shape=out,
            in_specs=[smem] * scalars + [vmem] * (len(args) - scalars),
            out_specs=vmem,
            scratch_shapes=list(scratch),
            compiler_params=pltpu.CompilerParams(vmem_limit_bytes=24 * 2**20),
            name=name,
        )(*args)

    return call


def reversed_table(table):
    turned = table[:, ::-1]
    return jnp.pad(turned, ((0, 0), (0, BLOCK - turned.shape[1])))


def bias_blocks(table):
    length = (table.shape[1] + 1) // 2
    shape = jax.ShapeDtypeStruct((PAIRS, BLOCK, 2 * BLOCK), F32)
    return whole(functools.partial(bias_kernel, length), shape, f"bias_{length}")(
        reversed_table(table)
    )


def exchange(array, axes):
    return lax.all_to_all(array, axes, split_axis=0, concat_axis=0, tiled=True)


def swap(array, axis):
    return lax.ppermute(array, axis, [(0, 1), (1, 0)])


def together(array, other):
    return lax.optimization_barrier((array, other))[0]


def shards(tokens, w_qkv, w_out, bias_x, bias_y, bias_z):
    features = tokens.shape[-1]
    shape = tokens.shape
    yh, yl = lax.axis_index("yh"), lax.axis_index("yl")
    x, c = lax.axis_index("x"), lax.axis_index("c")
    pair = yl * DIMS[3] + x
    peers = DIMS[0] * DIMS[1]
    zs = DIMS[2] * DIMS[3] * DIMS[4]

    depth = w_qkv.shape[0] // 2
    mine = [
        lax.dynamic_slice(w_qkv, (c * depth, part * features + pair * BLOCK), (depth, BLOCK))
        for part in range(3)
    ]
    mine.append(lax.dynamic_slice(w_out, (c * depth, pair * BLOCK), (depth, BLOCK)))
    mine = jnp.concatenate(mine, axis=1)
    piece = exchange(jnp.broadcast_to(mine[None], (DIMS[1], *mine.shape)), "z")
    piece = piece.reshape(DIMS[1] * depth, 4 * BLOCK)
    flat = tokens.reshape(-1, features)
    rows = flat.shape[0]
    normed = whole(norm_kernel, jax.ShapeDtypeStruct(flat.shape, BF), "norm")(flat)
    blocks_x = bias_blocks(bias_x)
    blocks_y = bias_blocks(bias_y)
    blocks_z = bias_blocks(bias_z)
    normed = together(normed, (blocks_x, blocks_y, blocks_z))
    piece = together(piece, normed)

    y_lines = exchange(normed.reshape(peers, -1, features), GY).reshape(rows, features)
    z_lines = exchange(together(normed, y_lines).reshape(zs, -1, features), GZ)
    z_lines = z_lines.reshape(rows, features)

    tall = piece.shape[0] // 2
    kept = jnp.where(c == 0, piece[:tall], piece[tall:])
    taken = swap(jnp.where(c == 0, piece[tall:], piece[:tall]), "c")
    rows_of = [jnp.where(c == 0, kept, taken), jnp.where(c == 0, taken, kept)]
    rows_of = [r.reshape(-1, depth, 4 * BLOCK) for r in rows_of]
    piece = jnp.stack(rows_of, axis=1).reshape(-1, 4 * BLOCK)
    first = [piece] + [lax.ppermute(piece, ALL, hop_plane(k, 0)) for k in range(1, 4)]
    first = jnp.stack([first[k] for k in HOPS])
    second = [first] + [lax.ppermute(first, ALL, hop_plane(k, 1)) for k in range(1, 4)]
    waits = {1: y_lines, 2: z_lines}
    others = [
        swap(together(second[k], waits[k]) if k in waits else second[k], "c") for k in range(4)
    ]

    columns = (x - jnp.array(HOPS)) % DIMS[3]
    y = yh * 2 + yl
    turned_b = ((y - 1) % 4) // 2
    scalars = jnp.concatenate(
        [yl * 4 + columns, (1 - yl) * 4 + columns, jnp.stack([c, yh, turned_b, yl, x])]
    ).astype(jnp.int32)

    every = (*second, *others)
    along_y, z = attend((2, 3), (y_lines, z_lines), every, (blocks_y, blocks_z), scalars)
    along_y = exchange(along_y.reshape(peers, -1, features), GY).reshape(rows, features)

    made = z
    z = z.reshape(4, rows // 4, features)
    back = [z[0]] + [lax.ppermute(z[k], ALL, hop_x(k)) for k in range(1, 4)]
    (along_x,) = attend((1,), (normed,), every, (blocks_x,), scalars)
    w_whole = gather_out(scalars, every, made)
    far_c = swap(jnp.stack([b[48:] for b in back]), "c")
    back_y = jnp.concatenate([jnp.stack([b[32:48] for b in back]), far_c], axis=0)
    back_y = swap(back_y, "yl")
    near_c = swap(jnp.stack([b[16:32] for b in back]), "c")
    near_z = jnp.concatenate([jnp.stack([b[:16] for b in back]), near_c], axis=0)
    mixed = mix(0, (rows // 2, features), scalars, flat, along_x, along_y, near_z, w_whole)
    mixed = mix(1, flat.shape, scalars, flat, along_x, along_y, back_y, w_whole, mixed)
    return mixed.reshape(shape)


def solution(mesh):
    torus = Mesh(mesh.devices.reshape(DIMS), ALL)
    in_specs = (P(None, None, GY, GZ, None), P(GY, None), P(GY, None), P(), P(), P())
    return jax.shard_map(
        shards, mesh=torus, in_specs=in_specs, out_specs=in_specs[0], check_vma=False
    )
```

```python
import functools
import jax
import jax.numpy as jnp
from jax import lax
from jax.experimental import pallas as pl
from jax.experimental.pallas import tpu as pltpu
from jax.sharding import Mesh
from jax.sharding import PartitionSpec as P

HEADS = 16
HEAD = 64
PAIRS = HEADS // 2
BLOCK = 128
NEG = -1e30
HOPS = (0, 2, 1, 3)
DIMS = (2, 16, 2, 4, 2)
ALL = ("yh", "z", "yl", "x", "c")
GY = ("yh", "z")
GZ = ("yl", "x", "c")
BF = jnp.bfloat16
F32 = jnp.float32


def index_of(yh, z, yl, x, c):
    return (((yh * DIMS[1] + z) * DIMS[2] + yl) * DIMS[3] + x) * DIMS[4] + c


def every_device():
    for yh in range(DIMS[0]):
        for z in range(DIMS[1]):
            for yl in range(DIMS[2]):
                for x in range(DIMS[3]):
                    for c in range(DIMS[4]):
                        yield yh, z, yl, x, c


def hop_x(far):
    return [
        (index_of(*d), index_of(d[0], d[1], d[2], (d[3] + far) % DIMS[3], d[4]))
        for d in every_device()
    ]


def hop_plane(far, x_core):
    pairs = []
    for yh, z, yl, x, c in every_device():
        y = yh * 2 + yl
        if c == x_core:
            x_to, y_to = (x + far) % 4, y
        else:
            x_to, y_to = x, (y + far) % 4
        pairs.append((index_of(yh, z, yl, x, c), index_of(y_to // 2, z, y_to % 2, x_to, c)))
    return pairs


def iota(shape, dim):
    return lax.broadcasted_iota(jnp.int32, shape, dim)


def line_rows(axis, i):
    if axis == 1:
        return (i & 128) + (i & 63) * 2 + ((i >> 6) & 1)
    if axis == 2:
        return (i & 31) * 8 + (i >> 5)
    return ((i & 30) << 3) + ((i >> 5) << 1) + (i & 1)


def norm_kernel(tokens_ref, out_ref):
    values = tokens_ref[...].astype(F32)
    center = jnp.mean(values, axis=-1, keepdims=True)
    values = values - center
    spread = jnp.mean(values * values, axis=-1, keepdims=True)
    out_ref[...] = (values * lax.rsqrt(spread + 1e-05)).astype(BF)


def bias_kernel(length, table_ref, out_ref):
    lanes = iota((length, BLOCK), 1) // length
    for head in range(HEADS):
        row = jnp.broadcast_to(table_ref[head : head + 1, :], (length, BLOCK))
        for place in range(BLOCK // length):
            shift = (place * length - length + 1) % BLOCK
            turned = pltpu.roll(row, shift, 1, stride=1, stride_axis=0)
            out_ref[
                head // 2,
                place * length : (place + 1) * length,
                (head % 2) * BLOCK : (head % 2 + 1) * BLOCK,
            ] = jnp.where(lanes == place, turned, NEG)


def attend_kernel(axes, scalar_ref, *refs):
    count = len(axes)
    token_refs, refs = refs[:count], refs[count:]
    weight_refs, refs = refs[:8], refs[8:]
    bias_refs = refs[: 2 * count]
    outs = sum(4 if axis == 3 else 1 for axis in axes)
    refs = refs[-(outs + count + 3) :]
    out_refs, back_refs = refs[:outs], refs[outs : outs + count]
    lines_ref, qkv_ref, mixed_ref = refs[outs + count :]
    step = pl.program_id(0)
    rows = token_refs[0].shape[0]
    core, turned_a, turned_b, yl, x = [scalar_ref[8 + n] for n in range(5)]

    @pl.when(step == 0)
    def _():
        for a, axis in enumerate(axes):
            turn = line_rows(axis, iota((rows, 1), 0)) == iota((rows, rows), 1)
            turn = turn.astype(F32).astype(BF)
            lines = jnp.dot(turn, token_refs[a][...], preferred_element_type=F32)
            lines_ref[a * rows : (a + 1) * rows] = lines.astype(BF)
            place = iota((rows, 1), 0)
            if axis == 3:
                dx, dy, dc = place >> 6, (place >> 5) & 1, (place >> 4) & 1
                to = (yl ^ dy) * 8 + ((x + dx) & 3) * 2 + (core ^ dc)
                back = ((place >> 1) & 7) * 32 + to * 2 + (place & 1) == iota((rows, rows), 1)
            else:
                back = line_rows(axis, iota((1, rows), 1)) == iota((rows, rows), 0)
            back_refs[a][...] = back.astype(F32).astype(BF)

    width = 3 * BLOCK

    def attention():
        left = iota((BLOCK, BLOCK), 1) < HEAD
        zero = jnp.zeros((BLOCK, BLOCK), BF)
        projected = (step + 1) % 2
        for n in range(2):
            pair = scalar_ref[2 * jnp.maximum(step - 1, 0) + n]
            columns = pl.ds(pl.multiple_of(pair * BLOCK, BLOCK), BLOCK)
            for start in range(0, count * rows, BLOCK):
                q, k, v = [
                    qkv_ref[
                        projected,
                        start : start + BLOCK,
                        n * width + m * BLOCK : n * width + (m + 1) * BLOCK,
                    ]
                    for m in range(3)
                ]
                keys = jnp.concatenate([jnp.where(left, k, zero), jnp.where(left, zero, k)], axis=0)
                values = jnp.concatenate([jnp.where(left, v, zero), jnp.where(left, zero, v)], axis=0)
                scores = lax.dot_general(q, keys, (((1,), (1,)), ((), ())), preferred_element_type=F32)
                scores = scores * HEAD ** (-0.5) + bias_refs[2 * (start // rows) + n][0]
                probs = []
                for half in range(2):
                    s = scores[:, half * BLOCK : (half + 1) * BLOCK]
                    e = jnp.exp(s - jnp.max(s, axis=-1, keepdims=True))
                    probs.append((e * (1.0 / jnp.sum(e, axis=-1, keepdims=True))).astype(BF))
                probs = jnp.concatenate(probs, axis=1)
                mixed = jnp.dot(probs, values, preferred_element_type=F32).astype(BF)
                mixed_ref[start : start + BLOCK, columns] = mixed

    def projection():
        turned = jnp.where(step < 2, turned_a, turned_b)
        near_first, far_first = step < 2, step % 2 == 0
        own_first = jnp.where(core == 0, near_first, far_first)
        other_first = jnp.where(core == 0, far_first, near_first)
        own_refs, other_refs = weight_refs[:4], weight_refs[4:]
        weights = []
        for n in range(2):
            halves = []
            for m in range(2):
                own, other = [
                    [jnp.where(early, part[2 * i][j], part[2 * i + 1][j]) for i, j in ((m, n), (n, m))]
                    for part, early in ((own_refs, own_first), (other_refs, other_first))
                ]
                near = jnp.where(core == 0, own[0], other[0])
                far = jnp.where(core == 0, other[1], own[1])
                halves.append(jnp.concatenate([near, far], axis=0))
            low = jnp.where(turned == 0, halves[0], halves[1])
            high = jnp.where(turned == 0, halves[1], halves[0])
            weights.append(jnp.concatenate([low, high], axis=0))
        weights = jnp.concatenate(weights, axis=1)
        qkv = jnp.dot(lines_ref[...], weights, preferred_element_type=F32)
        qkv_ref[step % 2] = qkv.astype(BF)

    last = pl.num_programs(0) - 1

    @pl.when(step == 0)
    def _():
        projection()

    @pl.when(jnp.logical_and(step > 0, step < last))
    def _():
        attention()
        projection()

    @pl.when(step == last)
    def _():
        attention()
        for a in range(count):
            mixed = mixed_ref[a * rows : (a + 1) * rows]
            out = jnp.dot(back_refs[a][...], mixed, preferred_element_type=F32)
            if axes[a] == 3:
                for k in range(4):
                    out_refs[a + k][...] = out[k * (rows // 4) : (k + 1) * (rows // 4)].astype(BF)
            else:
                out_refs[a][...] = out.astype(BF)


def attend(axes, tokens, weights, biases, scalars, after=()):
    rows, features = tokens[0].shape
    half, width = weights[0].shape[1], 3 * BLOCK
    count = len(axes)
    specs = [pl.BlockSpec((rows, features), lambda s, p: (0, 0))] * count

    for other in range(2):
        for hop in range(4):
            late = hop % 2

            def block(s, p, other=other, late=late):
                s = jnp.minimum(s, 3)
                y_part, x_part = s // 2, s % 2
                near = jnp.where(y_part == late, x_part, 1 - late)
                return (jnp.where(p[8] == other, near, y_part), 0, 0)

            specs.append(pl.BlockSpec((2, half, width), block))
    for _ in range(count):
        for n in range(2):

            def pair(s, p, n=n):
                return (p[2 * jnp.maximum(s - 1, 0) + n], 0, 0)

            specs.append(pl.BlockSpec((1, BLOCK, 2 * BLOCK), pair))
    specs.extend([pl.BlockSpec(memory_space=pl.ANY)] * len(after))
    heights = [n for axis in axes for n in ([rows // 4] * 4 if axis == 3 else [rows])]
    bias_args = [b for bias in biases for b in (bias, bias)]
    return pl.pallas_call(
        functools.partial(attend_kernel, axes),
        out_shape=[jax.ShapeDtypeStruct((n, features), BF) for n in heights],
        grid_spec=pltpu.PrefetchScalarGridSpec(
            num_scalar_prefetch=1,
            grid=(5,),
            in_specs=specs,
            out_specs=[pl.BlockSpec((n, features), lambda s, p: (0, 0)) for n in heights],
            scratch_shapes=[pltpu.VMEM((rows, rows), BF)] * count
            + [
                pltpu.VMEM((count * rows, features), BF),
                pltpu.VMEM((2, count * rows, 2 * width), BF),
                pltpu.VMEM((count * rows, features), BF),
            ],
        ),
        compiler_params=pltpu.CompilerParams(vmem_limit_bytes=61 * 2**20),
        cost_estimate=pl.CostEstimate(
            flops=10**10 if axes == (1,) else 1000, bytes_accessed=1000, transcendentals=0
        ),
        name="attend_" + "_".join(map(str, axes)),
    )(scalars, *tokens, *weights, *bias_args, *after)


def gather_kernel(scalar_ref, *refs):
    own_refs, other_refs, out_ref = refs[:4], refs[4:8], refs[-1]
    core, turned_a, turned_b = [scalar_ref[8 + n] for n in range(3)]
    for slot in range(PAIRS):
        group, k = slot // 4, slot % 4
        halves = []
        for m in (2 * group, 2 * group + 1):
            near = jnp.where(core == 0, own_refs[HOPS[m]][k], other_refs[HOPS[m]][k])
            far = jnp.where(core == 0, other_refs[HOPS[k]][m], own_refs[HOPS[k]][m])
            halves.append(jnp.concatenate([near, far], axis=0))
        turned = turned_b if group else turned_a
        low = jnp.where(turned == 0, halves[0], halves[1])
        high = jnp.where(turned == 0, halves[1], halves[0])
        columns = pl.ds(pl.multiple_of(scalar_ref[slot] * BLOCK, BLOCK), BLOCK)
        out_ref[:, columns] = jnp.concatenate([low, high], axis=0)


def gather_out(scalars, weights, after):
    half = weights[0].shape[1]
    size = HEADS * HEAD
    specs = [pl.BlockSpec((4, half, BLOCK), lambda i, p: (0, 0, 3))] * 8
    specs.append(pl.BlockSpec(memory_space=pl.ANY))
    return pl.pallas_call(
        gather_kernel,
        out_shape=jax.ShapeDtypeStruct((size, size), BF),
        grid_spec=pltpu.PrefetchScalarGridSpec(
            num_scalar_prefetch=1,
            grid=(1,),
            in_specs=specs,
            out_specs=pl.BlockSpec((size, size), lambda i, p: (0, 0)),
        ),
        compiler_params=pltpu.CompilerParams(vmem_limit_bytes=61 * 2**20),
        cost_estimate=pl.CostEstimate(flops=3 * 10**9, bytes_accessed=1000, transcendentals=0),
        name="gather_out",
    )(scalars, *weights, after)


def mix_kernel(distance, scalar_ref, tokens_ref, x_ref, y_ref, parts_ref, w_ref, *refs):
    out_ref, z_ref = refs[-2:]
    core, yl, x = scalar_ref[8], scalar_ref[11], scalar_ref[12]
    half = z_ref.shape[0]
    for k in range(4):
        for dc in range(2):
            source = ((x - k + 4) & 3) * 2 + (core ^ dc)
            z_ref[pl.ds(pl.multiple_of(source * 16, 16), 16), :] = parts_ref[dc * 4 + k]
    mine = pl.ds(pl.multiple_of((yl ^ distance) * half, half), half)
    summed = x_ref[mine, :].astype(F32) + y_ref[mine, :].astype(F32) + z_ref[...].astype(F32)
    result = jnp.dot(summed.astype(BF), w_ref[...], preferred_element_type=F32)
    result = (tokens_ref[mine, :].astype(F32) + result).astype(BF)
    if distance == 0:
        out_ref[...] = result
    else:
        out_ref[mine, :] = result
        out_ref[pl.ds(pl.multiple_of(yl * half, half), half), :] = refs[0][...]


def mix(distance, shape, scalars, *args):
    half = (args[0].shape[0] // 2, args[0].shape[1])
    return whole(
        functools.partial(mix_kernel, distance),
        jax.ShapeDtypeStruct(shape, BF),
        f"mix_{distance}",
        1,
        [pltpu.VMEM(half, BF)],
    )(scalars, *args)


def whole(kernel, out, name, scalars=0, scratch=()):
    vmem = pl.BlockSpec(memory_space=pltpu.VMEM)
    smem = pl.BlockSpec(memory_space=pltpu.SMEM)

    def call(*args):
        return pl.pallas_call(
            kernel,
            out_shape=out,
            in_specs=[smem] * scalars + [vmem] * (len(args) - scalars),
            out_specs=vmem,
            scratch_shapes=list(scratch),
            compiler_params=pltpu.CompilerParams(vmem_limit_bytes=24 * 2**20),
            name=name,
        )(*args)

    return call


def reversed_table(table):
    turned = table[:, ::-1]
    return jnp.pad(turned, ((0, 0), (0, BLOCK - turned.shape[1])))


def bias_blocks(table):
    length = (table.shape[1] + 1) // 2
    shape = jax.ShapeDtypeStruct((PAIRS, BLOCK, 2 * BLOCK), F32)
    return whole(functools.partial(bias_kernel, length), shape, f"bias_{length}")(
        reversed_table(table)
    )


def exchange(array, axes):
    return lax.all_to_all(array, axes, split_axis=0, concat_axis=0, tiled=True)


def swap(array, axis):
    return lax.ppermute(array, axis, [(0, 1), (1, 0)])


def together(array, other):
    return lax.optimization_barrier((array, other))[0]


def shards(tokens, w_qkv, w_out, bias_x, bias_y, bias_z):
    features = tokens.shape[-1]
    shape = tokens.shape
    yh, yl = lax.axis_index("yh"), lax.axis_index("yl")
    x, c = lax.axis_index("x"), lax.axis_index("c")
    pair = yl * DIMS[3] + x
    peers = DIMS[0] * DIMS[1]
    zs = DIMS[2] * DIMS[3] * DIMS[4]

    depth = w_qkv.shape[0] // 2
    mine = [
        lax.dynamic_slice(w_qkv, (c * depth, part * features + pair * BLOCK), (depth, BLOCK))
        for part in range(3)
    ]
    mine.append(lax.dynamic_slice(w_out, (c * depth, pair * BLOCK), (depth, BLOCK)))
    mine = jnp.concatenate(mine, axis=1)
    piece = exchange(jnp.broadcast_to(mine[None], (DIMS[1], *mine.shape)), "z")
    piece = piece.reshape(DIMS[1] * depth, 4 * BLOCK)
    flat = tokens.reshape(-1, features)
    rows = flat.shape[0]
    normed = whole(norm_kernel, jax.ShapeDtypeStruct(flat.shape, BF), "norm")(flat)
    blocks_x = bias_blocks(bias_x)
    blocks_y = bias_blocks(bias_y)
    blocks_z = bias_blocks(bias_z)
    normed = together(normed, (blocks_x, blocks_y, blocks_z))
    piece = together(piece, normed)

    y_lines = exchange(normed.reshape(peers, -1, features), GY).reshape(rows, features)
    z_lines = exchange(together(normed, y_lines).reshape(zs, -1, features), GZ)
    z_lines = z_lines.reshape(rows, features)

    tall = piece.shape[0] // 2
    kept = jnp.where(c == 0, piece[:tall], piece[tall:])
    taken = swap(jnp.where(c == 0, piece[tall:], piece[:tall]), "c")
    rows_of = [jnp.where(c == 0, kept, taken), jnp.where(c == 0, taken, kept)]
    rows_of = [r.reshape(-1, depth, 4 * BLOCK) for r in rows_of]
    piece = jnp.stack(rows_of, axis=1).reshape(-1, 4 * BLOCK)
    first = [piece] + [lax.ppermute(piece, ALL, hop_plane(k, 0)) for k in range(1, 4)]
    first = jnp.stack([first[k] for k in HOPS])
    second = [first] + [lax.ppermute(first, ALL, hop_plane(k, 1)) for k in range(1, 4)]
    waits = {1: y_lines, 2: z_lines}
    others = [
        swap(together(second[k], waits[k]) if k in waits else second[k], "c") for k in range(4)
    ]

    columns = (x - jnp.array(HOPS)) % DIMS[3]
    y = yh * 2 + yl
    turned_b = ((y - 1) % 4) // 2
    scalars = jnp.concatenate(
        [yl * 4 + columns, (1 - yl) * 4 + columns, jnp.stack([c, yh, turned_b, yl, x])]
    ).astype(jnp.int32)

    every = (*second, *others)
    along_y, *z = attend((2, 3), (y_lines, z_lines), every, (blocks_y, blocks_z), scalars)
    along_y = exchange(along_y.reshape(peers, -1, features), GY).reshape(rows, features)

    made = z[0]
    back = [z[0]] + [lax.ppermute(z[k], ALL, hop_x(k)) for k in range(1, 4)]
    (along_x,) = attend((1,), (normed,), every, (blocks_x,), scalars)
    w_whole = gather_out(scalars, every, made)
    far_c = swap(jnp.stack([b[48:] for b in back]), "c")
    back_y = jnp.concatenate([jnp.stack([b[32:48] for b in back]), far_c], axis=0)
    back_y = swap(back_y, "yl")
    near_c = swap(jnp.stack([b[16:32] for b in back]), "c")
    near_z = jnp.concatenate([jnp.stack([b[:16] for b in back]), near_c], axis=0)
    mixed = mix(0, (rows // 2, features), scalars, flat, along_x, along_y, near_z, w_whole)
    mixed = mix(1, flat.shape, scalars, flat, along_x, along_y, back_y, w_whole, mixed)
    return mixed.reshape(shape)


def solution(mesh):
    torus = Mesh(mesh.devices.reshape(DIMS), ALL)
    in_specs = (P(None, None, GY, GZ, None), P(GY, None), P(GY, None), P(), P(), P())
    return jax.shard_map(
        shards, mesh=torus, in_specs=in_specs, out_specs=in_specs[0], check_vma=False
    )
```
